128 devices in a mesh: row: 16 (over z, x), col: 8 (over y, core).
Axes of the slice: x: 4, y: 4, z: 4, core: 2. Of those that a mesh axis runs over, the one named last changes fastest.
Arguments:
- front_tiles: float32 [2, 16, 256, 4, 8, 256], P(None, 'row', None, None, 'col'), as said below
- child_tiles: float32 [16, 8, 16, 256, 256], P('row', 'col'), may hold values from -4 to 4
- child_target: int32 [16, 8, 16, 2], P('row', 'col'), may hold values from 0 to 31, as said below
- panel_tiles: int32 [2, 2], replicated, may hold values from 0 to 31, as said below
Outputs:
- factored: float32 [2, 16, 256, 4, 8, 256], P(None, 'row', None, None, 'col')
The draws below stay inside these ranges and needn't reach their ends.
Inputs may be any that keep to these rules, and one draw needn't show every extreme that they name: `child_target`: child tile number d + q of the device in grid row r targets a parent tile row d + 16 * a and a parent tile column (r % 8) + 8 * b, with a < 2 and b < 4. `panel_tiles`: all 4 entries differ. `front_tiles`: with the children's tiles added and all earlier panels' updates applied, every 512 pivot block has a positive diagonal, and the rest of the block has spectral norm under 0.8 times its smallest diagonal entry.
All inputs are finite; a program needn't handle non-finite values.
Results may differ from the reference program's by a relative error of at most 0.0001.
Values sent between devices are 32-bit elements; how exact they have to be, the bound alone decides.
A program may use at most 192 MiB of HBM per device.

```python
import jax
import jax.numpy as jnp
from jax import lax

TILE = 256
F = 8192
PANELS = 2
KR = 1
TILES = 32
TRD = 2
TCD = 4
N_ROW = 16
N_COL = 8


def pivot_order(key):
    own_key = jax.random.fold_in(key, 31)
    middle = jax.random.permutation(own_key, jnp.arange(1, TILES - 1, dtype=jnp.int32))[:2 * PANELS - 2]
    ends = jnp.array([0, TILES - 1], dtype=jnp.int32)
    picked = jnp.concatenate([ends, middle.astype(jnp.int32)])
    return jax.random.permutation(jax.random.fold_in(own_key, 3), picked).astype(jnp.int32)


def pivot_flags(key):
    chosen = pivot_order(key)
    return jnp.any(jnp.arange(TILES, dtype=jnp.int32)[:, None] == chosen[None, :], axis=1)


def target_tiles(key):
    own_key = jax.random.fold_in(key, 23)
    shape = (N_ROW, N_COL, N_ROW, KR)
    row_steps = jax.random.randint(own_key, shape, 0, TRD)
    col_steps = jax.random.randint(jax.random.fold_in(own_key, 7), shape, 0, TCD)
    source_rows = lax.broadcasted_iota(jnp.int32, shape, 0)
    group_rows = lax.broadcasted_iota(jnp.int32, shape, 2)
    parent_rows = group_rows + N_ROW * row_steps
    parent_cols = source_rows % N_COL + N_COL * col_steps
    stacked = jnp.stack([parent_rows, parent_cols], axis=-1)
    return stacked.reshape(N_ROW, N_COL, N_ROW * KR, 2).astype(jnp.int32)


def draw_front_tiles(key, part):
    flags = pivot_flags(key)
    key = jax.random.fold_in(key, 11)
    shape = (TRD, N_ROW, TILE, TCD, N_COL, TILE)
    pivot_rows = flags.reshape(TRD, N_ROW)[:, :, None, None, None, None]
    values = jax.random.normal(key, shape, jnp.float32)
    global_rows = (lax.broadcasted_iota(jnp.int32, shape, 0) * N_ROW + lax.broadcasted_iota(jnp.int32, shape, 1)) * TILE + lax.broadcasted_iota(jnp.int32, shape, 2)
    global_cols = (lax.broadcasted_iota(jnp.int32, shape, 3) * N_COL + lax.broadcasted_iota(jnp.int32, shape, 4)) * TILE + lax.broadcasted_iota(jnp.int32, shape, 5)
    boosts = 160.0 * (1.0 + 0.25 * jax.random.uniform(jax.random.fold_in(key, 5), shape, jnp.float32, -1.0, 1.0))
    entries = jnp.where((global_rows == global_cols) & pivot_rows, boosts, values)
    return jnp.where(pivot_rows, entries / 64.0, entries)


def draw_child_tiles(key, part):
    flags = pivot_flags(key)
    targets = target_tiles(key)
    key = jax.random.fold_in(key, 41)
    shape = (N_ROW, N_COL, N_ROW * KR, TILE, TILE)
    values = 0.5 * jax.random.truncated_normal(key, -8.0, 8.0, shape, jnp.float32)
    landing_pivot = jnp.take(flags, targets[..., 0])
    factors = jnp.where(landing_pivot, 1.0 / 64.0, 1.0).astype(jnp.float32)
    return values * factors[..., None, None]


def draw_child_target(key, part):
    return target_tiles(key)


def draw_panel_tiles(key, part):
    return pivot_order(key).reshape(PANELS, 2).astype(jnp.int32)


def setup_inputs(seed: int = 0) -> dict:
    seeds = jax.random.split(jax.random.key(seed), 5)
    front_tiles = draw_front_tiles(jax.random.fold_in(seeds[4], 71), 0)
    child_tiles = draw_child_tiles(jax.random.fold_in(seeds[4], 71), 0)
    child_target = draw_child_target(jax.random.fold_in(seeds[4], 71), 0)
    panel_tiles = draw_panel_tiles(jax.random.fold_in(seeds[4], 71), 0)
    return {"front_tiles": front_tiles, "child_tiles": child_tiles, "child_target": child_target, "panel_tiles": panel_tiles}


def reference(front_tiles, child_tiles, child_target, panel_tiles):
    grid = front_tiles.reshape(TILES, TILE, TILES, TILE).transpose(0, 2, 1, 3)
    flattened = child_tiles.reshape(-1, TILE, TILE)
    target_rows = child_target[..., 0].reshape(-1)
    target_cols = child_target[..., 1].reshape(-1)
    grid = grid.at[target_rows, target_cols].add(flattened)
    matrix = grid.transpose(0, 2, 1, 3).reshape(F, F)
    finished = jnp.zeros((TILES,), dtype=bool)
    tile_numbers = jnp.arange(TILES, dtype=jnp.int32)
    offsets = jnp.arange(TILE, dtype=jnp.int32)
    for panel_index in range(PANELS):
        chosen = panel_tiles[panel_index]
        finished = finished | (tile_numbers == chosen[0]) | (tile_numbers == chosen[1])
        trailing = jnp.repeat(jnp.logical_not(finished), TILE)
        positions = (chosen[:, None] * TILE + offsets[None, :]).reshape(-1).astype(jnp.int32)
        columns = matrix[:, positions]
        upper_rows = matrix[positions, :]
        pivot_block = columns[positions, :]
        lower_part = jnp.linalg.solve(pivot_block.T, columns.T).T
        lower_part = jnp.where(trailing[:, None], lower_part, 0.0)
        upper_part = jnp.where(trailing[None, :], upper_rows, 0.0)
        matrix = matrix - jnp.dot(lower_part, upper_part, precision=lax.Precision.HIGHEST)
        matrix = matrix.at[:, positions].set(jnp.where(trailing[:, None], lower_part, columns))
    return matrix.reshape(TRD, N_ROW, TILE, TCD, N_COL, TILE)
```

```python
import jax
import jax.numpy as jnp
from jax import lax
from jax.experimental import pallas as pl
from jax.experimental.pallas import tpu as pltpu
from jax.sharding import PartitionSpec as P

MESH = pl.DeviceIdType.MESH
DMA = pltpu.SemaphoreType.DMA
ANY = pl.BlockSpec(memory_space=pl.ANY)
VMEM = pl.BlockSpec(memory_space=pltpu.VMEM)
SMEM = pl.BlockSpec(memory_space=pltpu.SMEM)
F32 = jnp.float32
BF16 = jnp.bfloat16

PLANE = (
    (0, 1), (1, 0), (0, 3), (3, 0), (1, 1), (3, 3), (1, 3), (3, 1),
    (0, 2), (2, 0), (1, 2), (2, 1), (3, 2), (2, 3), (2, 2),
)
COLUMN = ((0, 1), (1, 0), (3, 0), (1, 1), (3, 1), (2, 0), (2, 1))
STEP = (1, 3, 2)
LOOSE_STEPS = 4
TIGHT_STEPS = 2


class Place:
    def __init__(self):
        self.r = lax.axis_index("row")
        self.c = lax.axis_index("col")
        self.z, self.x = self.r // 4, self.r % 4
        self.y, self.k = self.c // 2, self.c % 2

    def row(self, dz, dx):
        return (self.z + dz + 4) % 4 * 4 + (self.x + dx + 4) % 4

    def col(self, dy, dk):
        return (self.y + dy + 4) % 4 * 2 + (self.k + dk + 2) % 2


def remote(src, dst, send, recv, device):
    return pltpu.make_async_remote_copy(
        src_ref=src, dst_ref=dst, send_sem=send, recv_sem=recv, device_id=device, device_id_type=MESH
    )


def greet(me):
    barrier = pltpu.get_barrier_semaphore()
    for dz, dx in PLANE:
        pl.semaphore_signal(barrier, inc=1, device_id=(me.row(dz, dx), me.c), device_id_type=MESH)
    for dy, dk in COLUMN:
        pl.semaphore_signal(barrier, inc=1, device_id=(me.r, me.col(dy, dk)), device_id_type=MESH)
    pl.semaphore_wait(barrier, len(PLANE) + len(COLUMN))


def child_kernel(
    tiles, spots, out, out_spots, mid, mid_spots,
    own_sem, own_spot_sem, send1, recv1, spot_send1, spot_recv1, send2, recv2, spot_send2, spot_recv2,
):
    me = Place()
    greet(me)

    def first(index):
        dz, dx = PLANE[index]
        target = me.row(dz, dx)
        return (
            remote(tiles.at[target], mid.at[me.r], send1.at[index], recv1.at[index], (target, me.c)),
            remote(
                spots, mid_spots.at[me.r], spot_send1.at[index], spot_recv1.at[index], (target, me.c)
            ),
        )

    def second(source, index, tile, spot):
        col = source % 8
        half = source // 8
        place = half * 8 + me.c
        here = (
            pltpu.make_async_copy(tile, out.at[place], own_sem.at[half]),
            pltpu.make_async_copy(spot, out_spots.at[place], own_spot_sem.at[half]),
        )
        there = (
            remote(tile, out.at[place], send2.at[index], recv2.at[place], (me.r, col)),
            remote(spot, out_spots.at[place], spot_send2.at[index], spot_recv2.at[place], (me.r, col)),
        )
        return col, here, there

    def pass_on(source, index, tile, spot):
        col, here, there = second(source, index, tile, spot)

        @pl.when(col == me.c)
        def _():
            for copy in here:
                copy.start()

        @pl.when(col != me.c)
        def _():
            for copy in there:
                copy.start()

    def finish(source, index, tile, spot):
        col, here, there = second(source, index, tile, spot)

        @pl.when(col == me.c)
        def _():
            for copy in here:
                copy.wait()

        @pl.when(col != me.c)
        def _():
            for copy in there:
                copy.wait_send()

    last = len(PLANE)
    for index in range(last):
        for copy in first(index):
            copy.start()
    pass_on(me.r, last, tiles.at[me.r], spots)
    for index, (dz, dx) in enumerate(PLANE):
        source = me.row(-dz, -dx)
        for copy in first(index):
            copy.wait_recv()
        pass_on(source, index, mid.at[source], mid_spots.at[source])
    for index, (dz, dx) in enumerate(PLANE):
        for copy in first(index):
            copy.wait_send()
        source = me.row(-dz, -dx)
        finish(source, index, mid.at[source], mid_spots.at[source])
    finish(me.r, last, tiles.at[me.r], spots)
    for place in range(16):

        @pl.when(me.c != place % 8)
        def _():
            remote(
                out.at[place], out.at[place], send2.at[0], recv2.at[place], (me.r, me.c)
            ).wait_recv()
            remote(
                out_spots.at[place], out_spots.at[place], spot_send2.at[0], spot_recv2.at[place],
                (me.r, me.c),
            ).wait_recv()


def exchange_children(tiles, spots):
    return pl.pallas_call(
        child_kernel,
        name="children",
        out_shape=[
            jax.ShapeDtypeStruct((16, 256, 256), F32),
            jax.ShapeDtypeStruct((16, 8, 128), jnp.int32),
            jax.ShapeDtypeStruct((16, 256, 256), F32),
            jax.ShapeDtypeStruct((16, 8, 128), jnp.int32),
        ],
        in_specs=[ANY, ANY],
        out_specs=[ANY] * 4,
        scratch_shapes=[DMA((2,)), DMA((2,))] + [DMA((16,))] * 8,
        compiler_params=pltpu.CompilerParams(collective_id=0, has_side_effects=True),
    )(tiles, spots)[:2]


def extend_kernel(spots, front, tile, out):
    step = pl.program_id(0)

    @pl.when(step == 0)
    def _():
        out[...] = front[...]

    spot = spots[step]
    out[spot // 4, spot % 4] += tile[0]


def extend_add(spots, front, tiles):
    return pl.pallas_call(
        extend_kernel,
        name="extend",
        out_shape=jax.ShapeDtypeStruct((2, 4, 256, 256), F32),
        grid_spec=pltpu.PrefetchScalarGridSpec(
            num_scalar_prefetch=1,
            grid=(16,),
            in_specs=[
                pl.BlockSpec((2, 4, 256, 256), lambda i, s: (0, 0, 0, 0)),
                pl.BlockSpec((1, 256, 256), lambda i, s: (i, 0, 0)),
            ],
            out_specs=pl.BlockSpec((2, 4, 256, 256), lambda i, s: (0, 0, 0, 0)),
        ),
        compiler_params=pltpu.CompilerParams(vmem_limit_bytes=32 * 2**20),
    )(spots, front, tiles)


def spread_kernel(m, rows, cols, own, row_send, row_recv, col_send, col_recv):
    me = Place()
    greet(me)

    def row_slice(target):
        return m.at[:, :, pl.ds(pl.multiple_of(target * 16, 16), 16), :]

    def col_slice(target):
        return m.at[target // 4, :, pl.ds(pl.multiple_of(target % 4 * 64, 64), 64), :]

    copies = []
    for index, (dz, dx) in enumerate(PLANE):
        target = me.row(dz, dx)
        source = me.row(-dz, -dx)
        sent = remote(row_slice(target), rows.at[me.r], row_send.at[index], row_recv.at[index], (target, me.c))
        sent.start()
        copies.append(sent)
    for index, (dy, dk) in enumerate(COLUMN):
        target = me.col(dy, dk)
        sent = remote(col_slice(target), cols.at[me.c], col_send.at[index], col_recv.at[index], (me.r, target))
        sent.start()
        copies.append(sent)
    mine = (
        pltpu.make_async_copy(row_slice(me.r), rows.at[me.r], own.at[0]),
        pltpu.make_async_copy(col_slice(me.c), cols.at[me.c], own.at[1]),
    )
    for copy in mine:
        copy.start()
    for copy in mine:
        copy.wait()
    for copy in copies:
        copy.wait()


def spread(m):
    return pl.pallas_call(
        spread_kernel,
        name="spread",
        out_shape=[
            jax.ShapeDtypeStruct((16, 2, 4, 16, 256), F32),
            jax.ShapeDtypeStruct((8, 4, 64, 256), F32),
        ],
        in_specs=[ANY],
        out_specs=[ANY] * 2,
        scratch_shapes=[DMA((2,)), DMA((15,)), DMA((15,)), DMA((7,)), DMA((7,))],
        compiler_params=pltpu.CompilerParams(collective_id=1, has_side_effects=True),
    )(m)


class PlaneGather:
    def __init__(self, me, at, own, x_first, sems):
        self.me, self.at, self.own, self.x_first = me, at, own, x_first
        self.send1, self.recv1, self.send2, self.recv2 = sems

    def number(self, one, two):
        return self.me.row(two, one) if self.x_first else self.me.row(one, two)

    def _first(self, index):
        step = STEP[index]
        return lambda source: remote(
            self.own, self.at(source), self.send1.at[index], self.recv1.at[index],
            (self.number(step, 0), self.me.c),
        )

    def _second(self, which, index):
        source = self.number(-STEP[which - 1] if which else 0, 0)
        block = self.at(source)
        slot = which * 3 + index
        return lambda landed: remote(
            block if which else self.own, self.at(landed), self.send2.at[slot], self.recv2.at[slot],
            (self.number(0, STEP[index]), self.me.c),
        )

    def start(self):
        for index in range(3):
            self._first(index)(self.me.r).start()

    def forward(self, which):
        if which:
            source = self.number(-STEP[which - 1], 0)
            self._first(which - 1)(source).wait_recv()
        else:
            source = self.me.r
        for index in range(3):
            self._second(which, index)(source).start()
        return source

    def arrive(self, which, index):
        source = self.number(-STEP[which - 1] if which else 0, -STEP[index])
        self._second(which, index)(source).wait_recv()
        return source

    def drain(self):
        for index in range(3):
            self._first(index)(self.me.r).wait_send()
        for which in range(4):
            for index in range(3):
                self._second(which, index)(self.me.r).wait_send()


def gather_kernel(
    panel, rows, cols, ug, bg, cg, upc, cpc, bsc, bpc, own,
    bs_s, bs_r, bc_s, bc_r, c_s, c_r, cx_s, cx_r, ua, ub, ba, bb, bx_s, bx_r,
):
    me = Place()
    greet(me)
    other = 1 - me.k
    pivots = [panel[j // 2, j % 2] for j in range(4)]
    for j, pivot in enumerate(pivots):
        upc[:, j] = rows[pivot % 16, pivot // 16]
        cpc[j] = cols[pivot % 8, pivot // 8]

    def b_rows(col):
        return upc.at[:, col // 2, pl.ds(pl.multiple_of(col % 2 * 8, 8), 8), :]

    def b_scatter(index):
        dy, dk = COLUMN[index]
        target = me.col(dy, dk)
        return lambda source: remote(
            b_rows(target), bsc.at[source], bs_s.at[index], bs_r.at[index], (me.r, target)
        )

    for index in range(7):
        b_scatter(index)(me.c).start()
    own_scatter = pltpu.make_async_copy(b_rows(me.c), bsc.at[me.c], own.at[0])
    own_scatter.start()

    def u_at(first):
        return lambda source: ug.at[:, pl.ds(first, 2), source]

    u1 = PlaneGather(me, u_at(0), upc.at[:, pl.ds(0, 2)], True, ua)
    u2 = PlaneGather(me, u_at(2), upc.at[:, pl.ds(2, 2)], False, ub)
    u1.start()
    u2.start()
    own_u = pltpu.make_async_copy(upc, ug.at[:, :, me.r], own.at[1])
    own_u.start()

    def c_out(index):
        step = STEP[index]
        return lambda source: remote(
            cpc, cg.at[source], c_s.at[index], c_r.at[index], (me.r, me.col(step, 0))
        )

    def c_swap(which):
        source = me.col(-STEP[which - 1] if which else 0, 0)
        src = cg.at[source] if which else cpc
        return lambda landed: remote(
            src, cg.at[landed], cx_s.at[which], cx_r.at[which], (me.r, me.col(0, 1))
        )

    for index in range(3):
        c_out(index)(me.c).start()
    c_swap(0)(me.c).start()
    own_c = pltpu.make_async_copy(cpc, cg.at[me.c], own.at[2])
    own_c.start()

    own_scatter.wait()
    for index, (dy, dk) in enumerate(COLUMN):
        b_scatter(index)(me.col(-dy, -dk)).wait_recv()
    for j, pivot in enumerate(pivots):
        bpc[j] = bsc[pivot % 8, pivot // 8]

    def b_piece(col):
        return bg.at[:, col // 2, me.r, pl.ds(pl.multiple_of(col % 2 * 8, 8), 8), :]

    def b_gather(index):
        dy, dk = COLUMN[index]
        return lambda source: remote(
            bpc, b_piece(source), bc_s.at[index], bc_r.at[index], (me.r, me.col(dy, dk))
        )

    for index in range(7):
        b_gather(index)(me.c).start()
    own_b = pltpu.make_async_copy(bpc, b_piece(me.c), own.at[3])
    own_b.start()
    own_b.wait()
    for index, (dy, dk) in enumerate(COLUMN):
        b_gather(index)(me.col(-dy, -dk)).wait_recv()

    def b_at(pivot):
        return lambda source: bg.at[:, pivot, source]

    b1 = PlaneGather(me, b_at(me.k), b_at(me.k)(me.r), True, ba)
    b2 = PlaneGather(me, b_at(2 + me.k), b_at(2 + me.k)(me.r), False, bb)
    b1.start()
    b2.start()

    def b_swap(half, slot, source, back):
        pivot = 2 * half + (other if back else me.k)
        block = bg.at[:, pivot, source]
        return remote(block, block, bx_s.at[half, slot], bx_r.at[half, slot], (me.r, me.col(0, 1)))

    for which in range(4):
        for half, gather in enumerate((b1, b2)):
            source = gather.forward(which)
            if which:
                b_swap(half, which - 1, source, False).start()
    for which in range(4):
        for gather in (u1, u2):
            gather.forward(which)
    for which in range(1, 4):
        source = me.col(-STEP[which - 1], 0)
        c_out(which - 1)(source).wait_recv()
        c_swap(which)(source).start()
    for which in range(4):
        for index in range(3):
            for half, gather in enumerate((b1, b2)):
                source = gather.arrive(which, index)
                b_swap(half, 3 + which * 3 + index, source, False).start()

    for which in range(4):
        for index in range(3):
            for gather in (u1, u2):
                gather.arrive(which, index)
    own_u.wait()
    own_c.wait()
    for which in range(4):
        c_swap(which)(me.col(-STEP[which - 1] if which else 0, 1)).wait_recv()
    for half, gather in enumerate((b1, b2)):
        for which in range(1, 4):
            source = gather.number(-STEP[which - 1], 0)
            b_swap(half, which - 1, source, True).wait_recv()
        for which in range(4):
            for index in range(3):
                source = gather.number(-STEP[which - 1] if which else 0, -STEP[index])
                b_swap(half, 3 + which * 3 + index, source, True).wait_recv()
    for index in range(7):
        b_scatter(index)(me.c).wait_send()
        b_gather(index)(me.c).wait_send()
    for index in range(3):
        c_out(index)(me.c).wait_send()
    for which in range(4):
        c_swap(which)(me.c).wait_send()
    for gather in (u1, u2, b1, b2):
        gather.drain()
    for half, gather in enumerate((b1, b2)):
        for slot in range(15):
            b_swap(half, slot, me.r, False).wait_send()


def gather_pivots(panel, rows, cols):
    plane = [DMA((3,)), DMA((3,)), DMA((12,)), DMA((12,))]
    return pl.pallas_call(
        gather_kernel,
        name="gather",
        out_shape=[
            jax.ShapeDtypeStruct((4, 4, 16, 16, 256), F32),
            jax.ShapeDtypeStruct((4, 4, 16, 16, 256), F32),
            jax.ShapeDtypeStruct((8, 4, 64, 256), F32),
        ],
        in_specs=[SMEM, VMEM, VMEM],
        out_specs=[ANY] * 3,
        scratch_shapes=[
            pltpu.VMEM((4, 4, 16, 256), F32),
            pltpu.VMEM((4, 64, 256), F32),
            pltpu.VMEM((8, 4, 8, 256), F32),
            pltpu.VMEM((4, 8, 256), F32),
            DMA((4,)),
            DMA((7,)), DMA((7,)), DMA((7,)), DMA((7,)),
            DMA((3,)), DMA((3,)), DMA((4,)), DMA((4,)),
            plane, plane, plane, plane,
            DMA((2, 15)), DMA((2, 15)),
        ],
        compiler_params=pltpu.CompilerParams(
            collective_id=2, has_side_effects=True, vmem_limit_bytes=32 * 2**20
        ),
    )(panel, rows, cols)


def split(value):
    high = value.astype(BF16)
    return high, (value - high.astype(F32)).astype(BF16)


def dot1(a, b):
    return jnp.dot(a, b, preferred_element_type=F32)


def dot3(a, b):
    return dot1(a[0], b[0]) + (dot1(a[0], b[1]) + dot1(a[1], b[0]))


def invert(block, block_high, block_low, estimate):
    size = block.shape[0]
    diagonal = lax.broadcasted_iota(jnp.int32, (size, size), 0) == lax.broadcasted_iota(
        jnp.int32, (size, size), 1
    )
    value = block[...]
    high, low = split(value)
    block_high[...] = high
    block_low[...] = low
    weights = jnp.sum(jnp.where(diagonal, value, 0.0), axis=0, keepdims=True)
    estimate[...] = jnp.where(diagonal, 1.0 / weights, 0.0)

    def loose(step, carry):
        now = estimate[...]
        high = now.astype(BF16)
        product = dot1(block_high[...], high)
        estimate[...] = 2.0 * now - dot1(high, product.astype(BF16))
        return carry

    def tight(step, carry):
        now = estimate[...]
        halves = split(now)
        product = dot3((block_high[...], block_low[...]), halves)
        estimate[...] = 2.0 * now - dot3(halves, split(product))
        return carry

    lax.fori_loop(0, LOOSE_STEPS, loose, 0)
    lax.fori_loop(0, TIGHT_STEPS, tight, 0)


def factor_kernel(panel, m, ug, bg, cg, out, block, block_high, block_low, x1, x2, l1, l2, c2, lt_high, lt_low):
    r = lax.axis_index("row")
    c = lax.axis_index("col")
    pivots = [panel[j // 2, j % 2] for j in range(4)]
    row_tile = (lax.broadcasted_iota(jnp.int32, (512, 1), 0) // 256) * 16 + r
    in1 = (row_tile == pivots[0]) | (row_tile == pivots[1])
    in2 = (row_tile == pivots[2]) | (row_tile == pivots[3])

    def b_part(rows, cols):
        return jnp.concatenate(
            [bg[2 * cols + j, pl.ds(2 * rows, 2)].reshape(512, 256) for j in range(2)], axis=1
        )

    def c_part(cols):
        return jnp.concatenate([cg[:, 2 * cols + j].reshape(512, 256) for j in range(2)], axis=1)

    block[...] = b_part(0, 0)
    invert(block, block_high, block_low, x1)
    x1_halves = split(x1[...])
    b12 = split(b_part(0, 1))
    t_halves = split(dot3(split(b_part(1, 0)), x1_halves))
    block[...] = b_part(1, 1) - dot3(t_halves, b12)
    lower = dot3(split(c_part(0)), x1_halves)
    l1[...] = lower
    lower = jnp.where(in1, 0.0, lower)
    c2[...] = c_part(1) - dot3(split(lower), b12)
    invert(block, block_high, block_low, x2)
    lower2 = dot3(split(c2[...]), split(x2[...]))
    l2[...] = lower2
    lower2 = jnp.where(in1 | in2, 0.0, lower2)
    halves = split(lower2)
    lt_high[:, 512:], lt_low[:, 512:] = halves
    lt_high[:, :512], lt_low[:, :512] = split(lower - dot3(halves, t_halves))
    for b in range(4):
        update = dot3((lt_high[...], lt_low[...]), split(ug[b].reshape(1024, 256)))
        col_tile = b * 8 + c
        new = m[:, b].reshape(512, 256) - update
        for j in range(4):
            cols = slice(j % 2 * 256, j % 2 * 256 + 256)
            if j < 2:
                column = jnp.where(in1, cg[:, j].reshape(512, 256), l1[:, cols])
            else:
                column = jnp.where(in1 | in2, c2[:, cols], l2[:, cols])
            new = jnp.where(col_tile == pivots[j], column, new)
        out[:, b] = new.reshape(2, 256, 256)


def factor(panel, m, ug, bg, cg):
    square = pltpu.VMEM((512, 512), F32)
    half = pltpu.VMEM((512, 512), BF16)
    return pl.pallas_call(
        factor_kernel,
        name="factor",
        out_shape=jax.ShapeDtypeStruct((2, 4, 256, 256), F32),
        in_specs=[SMEM] + [VMEM] * 4,
        out_specs=VMEM,
        scratch_shapes=[square, half, half] + [square] * 5 + [pltpu.VMEM((512, 1024), BF16)] * 2,
        compiler_params=pltpu.CompilerParams(vmem_limit_bytes=56 * 2**20),
    )(panel, m, ug, bg, cg)


def shards(front_tiles, child_tiles, child_target, panel_tiles):
    front = front_tiles.reshape(2, 256, 4, 256).transpose(0, 2, 1, 3)
    targets = child_target.reshape(16, 2)
    spots = targets[:, 0] // 16 * 4 + targets[:, 1] // 8
    spots = jnp.broadcast_to(jnp.pad(spots, (0, 112)), (8, 128))
    tiles, spot_blocks = exchange_children(child_tiles.reshape(16, 256, 256), spots)
    landed = lax.dynamic_slice_in_dim(spot_blocks[:, 0, :], lax.axis_index("row"), 1, axis=1)[:, 0]
    m = extend_add(landed, front, tiles)
    rows, cols = spread(m)
    ug, bg, cg = gather_pivots(panel_tiles, rows, cols)
    out = factor(panel_tiles, m, ug, bg, cg)
    return out.transpose(0, 2, 1, 3).reshape(front_tiles.shape)


def solution(mesh):
    in_specs = (
        P(None, "row", None, None, "col", None),
        P("row", "col", None, None, None),
        P("row", "col", None, None),
        P(),
    )
    out_specs = P(None, "row", None, None, "col", None)
    return jax.shard_map(shards, mesh=mesh, in_specs=in_specs, out_specs=out_specs, check_vma=False)
```

```python
import jax
import jax.numpy as jnp
from jax import lax
from jax.experimental import pallas as pl
from jax.experimental.pallas import tpu as pltpu
from jax.sharding import PartitionSpec as P

MESH = pl.DeviceIdType.MESH
DMA = pltpu.SemaphoreType.DMA
ANY = pl.BlockSpec(memory_space=pl.ANY)
VMEM = pl.BlockSpec(memory_space=pltpu.VMEM)
SMEM = pl.BlockSpec(memory_space=pltpu.SMEM)
F32 = jnp.float32
BF16 = jnp.bfloat16

PLANE = (
    (0, 1), (1, 0), (0, 3), (3, 0), (1, 1), (3, 3), (1, 3), (3, 1),
    (0, 2), (2, 0), (1, 2), (2, 1), (3, 2), (2, 3), (2, 2),
)
COLUMN = ((0, 1), (1, 0), (3, 0), (1, 1), (3, 1), (2, 0), (2, 1))
STEP = (1, 3, 2)
LOOSE_STEPS = 4
TIGHT_STEPS = 2


class Place:
    def __init__(self):
        self.r = lax.axis_index("row")
        self.c = lax.axis_index("col")
        self.z, self.x = self.r // 4, self.r % 4
        self.y, self.k = self.c // 2, self.c % 2

    def row(self, dz, dx):
        return (self.z + dz + 4) % 4 * 4 + (self.x + dx + 4) % 4

    def col(self, dy, dk):
        return (self.y + dy + 4) % 4 * 2 + (self.k + dk + 2) % 2


def remote(src, dst, send, recv, device):
    return pltpu.make_async_remote_copy(
        src_ref=src, dst_ref=dst, send_sem=send, recv_sem=recv, device_id=device, device_id_type=MESH
    )


def greet(me):
    barrier = pltpu.get_barrier_semaphore()
    for dz, dx in PLANE:
        pl.semaphore_signal(barrier, inc=1, device_id=(me.row(dz, dx), me.c), device_id_type=MESH)
    for dy, dk in COLUMN:
        pl.semaphore_signal(barrier, inc=1, device_id=(me.r, me.col(dy, dk)), device_id_type=MESH)
    pl.semaphore_wait(barrier, len(PLANE) + len(COLUMN))


def child_kernel(
    tiles, spots, out, out_spots, mid, mid_spots,
    own_sem, own_spot_sem, send1, recv1, spot_send1, spot_recv1, send2, recv2, spot_send2, spot_recv2,
):
    me = Place()
    greet(me)

    def first(index):
        dz, dx = PLANE[index]
        target = me.row(dz, dx)
        return (
            remote(tiles.at[target], mid.at[me.r], send1.at[index], recv1.at[index], (target, me.c)),
            remote(
                spots, mid_spots.at[me.r], spot_send1.at[index], spot_recv1.at[index], (target, me.c)
            ),
        )

    def second(source, index, tile, spot):
        col = source % 8
        half = source // 8
        place = half * 8 + me.c
        here = (
            pltpu.make_async_copy(tile, out.at[place], own_sem.at[half]),
            pltpu.make_async_copy(spot, out_spots.at[place], own_spot_sem.at[half]),
        )
        there = (
            remote(tile, out.at[place], send2.at[index], recv2.at[place], (me.r, col)),
            remote(spot, out_spots.at[place], spot_send2.at[index], spot_recv2.at[place], (me.r, col)),
        )
        return col, here, there

    def pass_on(source, index, tile, spot):
        col, here, there = second(source, index, tile, spot)

        @pl.when(col == me.c)
        def _():
            for copy in here:
                copy.start()

        @pl.when(col != me.c)
        def _():
            for copy in there:
                copy.start()

    def finish(source, index, tile, spot):
        col, here, there = second(source, index, tile, spot)

        @pl.when(col == me.c)
        def _():
            for copy in here:
                copy.wait()

        @pl.when(col != me.c)
        def _():
            for copy in there:
                copy.wait_send()

    last = len(PLANE)
    for index in range(last):
        for copy in first(index):
            copy.start()
    pass_on(me.r, last, tiles.at[me.r], spots)
    for index, (dz, dx) in enumerate(PLANE):
        source = me.row(-dz, -dx)
        for copy in first(index):
            copy.wait_recv()
        pass_on(source, index, mid.at[source], mid_spots.at[source])
    for index, (dz, dx) in enumerate(PLANE):
        for copy in first(index):
            copy.wait_send()
        source = me.row(-dz, -dx)
        finish(source, index, mid.at[source], mid_spots.at[source])
    finish(me.r, last, tiles.at[me.r], spots)
    for place in range(16):

        @pl.when(me.c != place % 8)
        def _():
            remote(
                out.at[place], out.at[place], send2.at[0], recv2.at[place], (me.r, me.c)
            ).wait_recv()
            remote(
                out_spots.at[place], out_spots.at[place], spot_send2.at[0], spot_recv2.at[place],
                (me.r, me.c),
            ).wait_recv()


def exchange_children(tiles, spots):
    return pl.pallas_call(
        child_kernel,
        name="children",
        out_shape=[
            jax.ShapeDtypeStruct((16, 256, 256), F32),
            jax.ShapeDtypeStruct((16, 8, 128), jnp.int32),
            jax.ShapeDtypeStruct((16, 256, 256), F32),
            jax.ShapeDtypeStruct((16, 8, 128), jnp.int32),
        ],
        in_specs=[ANY, ANY],
        out_specs=[ANY] * 4,
        scratch_shapes=[DMA((2,)), DMA((2,))] + [DMA((16,))] * 8,
        compiler_params=pltpu.CompilerParams(collective_id=0, has_side_effects=True),
    )(tiles, spots)[:2]


def extend_kernel(spots, front, tile, out):
    step = pl.program_id(0)

    @pl.when(step == 0)
    def _():
        for chunk in range(8):
            part = front[pl.ds(chunk, 512, stride=8), :].reshape(2, 256, 128)
            out[:, chunk // 2, :, pl.ds(chunk % 2 * 128, 128)] = part

    spot = spots[step, 0, lax.axis_index("row")]
    out[spot // 4, spot % 4] += tile[0]


def extend_add(spots, front, tiles):
    return pl.pallas_call(
        extend_kernel,
        name="extend",
        out_shape=jax.ShapeDtypeStruct((2, 4, 256, 256), F32),
        grid=(16,),
        in_specs=[SMEM, VMEM, pl.BlockSpec((1, 256, 256), lambda i: (i, 0, 0))],
        out_specs=pl.BlockSpec((2, 4, 256, 256), lambda i: (0, 0, 0, 0)),
        compiler_params=pltpu.CompilerParams(vmem_limit_bytes=32 * 2**20),
    )(spots, front, tiles)


class PlaneGather:
    def __init__(self, me, at, own, x_first, sems):
        self.me, self.at, self.own, self.x_first = me, at, own, x_first
        self.send1, self.recv1, self.send2, self.recv2 = sems

    def number(self, one, two):
        return self.me.row(two, one) if self.x_first else self.me.row(one, two)

    def _first(self, index):
        step = STEP[index]
        return lambda source: remote(
            self.own, self.at(source), self.send1.at[index], self.recv1.at[index],
            (self.number(step, 0), self.me.c),
        )

    def _second(self, which, index):
        source = self.number(-STEP[which - 1] if which else 0, 0)
        block = self.at(source)
        slot = which * 3 + index
        return lambda landed: remote(
            block if which else self.own, self.at(landed), self.send2.at[slot], self.recv2.at[slot],
            (self.number(0, STEP[index]), self.me.c),
        )

    def start(self):
        for index in range(3):
            self._first(index)(self.me.r).start()

    def forward(self, which):
        if which:
            source = self.number(-STEP[which - 1], 0)
            self._first(which - 1)(source).wait_recv()
        else:
            source = self.me.r
        for index in range(3):
            self._second(which, index)(source).start()
        return source

    def arrive(self, which, index):
        source = self.number(-STEP[which - 1] if which else 0, -STEP[index])
        self._second(which, index)(source).wait_recv()
        return source

    def drain(self):
        for index in range(3):
            self._first(index)(self.me.r).wait_send()
        for which in range(4):
            for index in range(3):
                self._second(which, index)(self.me.r).wait_send()


def split(value):
    high = value.astype(BF16)
    return high, (value - high.astype(F32)).astype(BF16)


def dot1(a, b):
    return jnp.dot(a, b, preferred_element_type=F32)


def dot3(a, b):
    return dot1(a[0], b[0]) + (dot1(a[0], b[1]) + dot1(a[1], b[0]))


def invert(block, block_high, block_low, estimate):
    size = block.shape[0]
    diagonal = lax.broadcasted_iota(jnp.int32, (size, size), 0) == lax.broadcasted_iota(
        jnp.int32, (size, size), 1
    )
    value = block[...]
    high, low = split(value)
    block_high[...] = high
    block_low[...] = low
    weights = jnp.sum(jnp.where(diagonal, value, 0.0), axis=0, keepdims=True)
    estimate[...] = jnp.where(diagonal, 1.0 / weights, 0.0)

    def loose(step, carry):
        now = estimate[...]
        high = now.astype(BF16)
        product = dot1(block_high[...], high)
        estimate[...] = 2.0 * now - dot1(high, product.astype(BF16))
        return carry

    def tight(step, carry):
        now = estimate[...]
        halves = split(now)
        product = dot3((block_high[...], block_low[...]), halves)
        estimate[...] = 2.0 * now - dot3(halves, split(product))
        return carry

    lax.fori_loop(0, LOOSE_STEPS, loose, 0)
    lax.fori_loop(0, TIGHT_STEPS, tight, 0)


def pivot_kernel(
    panel, m_in, out, m, rows, cols, ug, bg, cg, upc, cpc, bsc, bpc,
    block, block_high, block_low, x1, x2, l1, l2, c2, lt_high, lt_low, own,
    row_s, row_r, col_s, col_r, bs_s, bs_r, bc_s, bc_r, c_s, c_r, cx_s, cx_r, ua, ub, ba, bb, bx_s, bx_r,
):
    me = Place()
    greet(me)
    pivots = [panel[j // 2, j % 2] for j in range(4)]
    own_m = pltpu.make_async_copy(m_in, m, own.at[6])
    own_m.start()

    def row_slice(target):
        return m_in.at[:, :, pl.ds(pl.multiple_of(target * 16, 16), 16), :]

    def col_slice(target):
        return m_in.at[target // 4, :, pl.ds(pl.multiple_of(target % 4 * 64, 64), 64), :]

    def row_spread(index):
        target = me.row(*PLANE[index])
        return lambda source: remote(
            row_slice(target), rows.at[source], row_s.at[index], row_r.at[index], (target, me.c)
        )

    def col_spread(index):
        target = me.col(*COLUMN[index])
        return lambda source: remote(
            col_slice(target), cols.at[source], col_s.at[index], col_r.at[index], (me.r, target)
        )

    for index in range(15):
        row_spread(index)(me.r).start()
        if index < 7:
            col_spread(index)(me.c).start()
    mine = (
        pltpu.make_async_copy(row_slice(me.r), rows.at[me.r], own.at[0]),
        pltpu.make_async_copy(col_slice(me.c), cols.at[me.c], own.at[1]),
    )
    for copy in mine:
        copy.start()
    for copy in mine:
        copy.wait()
    for index, (dz, dx) in enumerate(PLANE):
        row_spread(index)(me.row(-dz, -dx)).wait_recv()
    for j, pivot in enumerate(pivots):
        upc[:, j] = rows[pivot % 16, pivot // 16]

    def b_rows(col):
        return upc.at[:, col // 2, pl.ds(pl.multiple_of(col % 2 * 8, 8), 8), :]

    def b_scatter(index):
        target = me.col(*COLUMN[index])
        return lambda source: remote(
            b_rows(target), bsc.at[source], bs_s.at[index], bs_r.at[index], (me.r, target)
        )

    for index in range(7):
        b_scatter(index)(me.c).start()
    own_scatter = pltpu.make_async_copy(b_rows(me.c), bsc.at[me.c], own.at[2])
    own_scatter.start()

    def u_at(first):
        return lambda source: ug.at[:, pl.ds(first, 2), source]

    u1 = PlaneGather(me, u_at(0), upc.at[:, pl.ds(0, 2)], True, ua)
    u2 = PlaneGather(me, u_at(2), upc.at[:, pl.ds(2, 2)], False, ub)
    u1.start()
    u2.start()
    own_u = pltpu.make_async_copy(upc, ug.at[:, :, me.r], own.at[3])
    own_u.start()

    own_scatter.wait()
    for index, (dy, dk) in enumerate(COLUMN):
        b_scatter(index)(me.col(-dy, -dk)).wait_recv()
    for j, pivot in enumerate(pivots):
        bpc[j] = bsc[pivot % 8, pivot // 8]

    def b_piece(col):
        return bg.at[:, col // 2, me.r, pl.ds(pl.multiple_of(col % 2 * 8, 8), 8), :]

    def b_gather(index):
        return lambda source: remote(
            bpc, b_piece(source), bc_s.at[index], bc_r.at[index], (me.r, me.col(*COLUMN[index]))
        )

    for index in range(7):
        b_gather(index)(me.c).start()
    own_b = pltpu.make_async_copy(bpc, b_piece(me.c), own.at[4])
    own_b.start()

    for index, (dy, dk) in enumerate(COLUMN):
        col_spread(index)(me.col(-dy, -dk)).wait_recv()
    for j, pivot in enumerate(pivots):
        cpc[j] = cols[pivot % 8, pivot // 8]

    def c_out(index):
        return lambda source: remote(
            cpc, cg.at[source], c_s.at[index], c_r.at[index], (me.r, me.col(STEP[index], 0))
        )

    def c_swap(which):
        source = me.col(-STEP[which - 1] if which else 0, 0)
        src = cg.at[source] if which else cpc
        return lambda landed: remote(
            src, cg.at[landed], cx_s.at[which], cx_r.at[which], (me.r, me.col(0, 1))
        )

    own_b.wait()
    for index, (dy, dk) in enumerate(COLUMN):
        b_gather(index)(me.col(-dy, -dk)).wait_recv()

    def b_at(pivot):
        return lambda source: bg.at[:, pivot, source]

    b1 = PlaneGather(me, b_at(me.k), b_at(me.k)(me.r), True, ba)
    b2 = PlaneGather(me, b_at(2 + me.k), b_at(2 + me.k)(me.r), False, bb)
    b1.start()
    b2.start()

    def b_swap(half, slot, source, back):
        pivot = 2 * half + (1 - me.k if back else me.k)
        block = bg.at[:, pivot, source]
        return remote(block, block, bx_s.at[half, slot], bx_r.at[half, slot], (me.r, me.col(0, 1)))

    for index in range(3):
        c_out(index)(me.c).start()
    c_swap(0)(me.c).start()
    own_c = pltpu.make_async_copy(cpc, cg.at[me.c], own.at[5])
    own_c.start()

    for which in range(4):
        for half, gather in enumerate((b1, b2)):
            source = gather.forward(which)
            if which:
                b_swap(half, which - 1, source, False).start()
    for which in range(4):
        for gather in (u1, u2):
            gather.forward(which)
    for which in range(1, 4):
        source = me.col(-STEP[which - 1], 0)
        c_out(which - 1)(source).wait_recv()
        c_swap(which)(source).start()
    for half, gather in enumerate((b1, b2)):
        for which in range(4):
            for index in range(3):
                source = gather.arrive(which, index)
                b_swap(half, 3 + which * 3 + index, source, False).start()

    def b_arrived(half, gather):
        for which in range(1, 4):
            source = gather.number(-STEP[which - 1], 0)
            b_swap(half, which - 1, source, True).wait_recv()
        for which in range(4):
            for index in range(3):
                source = gather.number(-STEP[which - 1] if which else 0, -STEP[index])
                b_swap(half, 3 + which * 3 + index, source, True).wait_recv()

    row_tile = (lax.broadcasted_iota(jnp.int32, (512, 1), 0) // 256) * 16 + me.r
    in1 = (row_tile == pivots[0]) | (row_tile == pivots[1])
    in2 = (row_tile == pivots[2]) | (row_tile == pivots[3])

    def b_part(rows, cols):
        return jnp.concatenate(
            [bg[2 * cols + j, pl.ds(2 * rows, 2)].reshape(512, 256) for j in range(2)], axis=1
        )

    def c_part(cols):
        return jnp.concatenate([cg[:, 2 * cols + j].reshape(512, 256) for j in range(2)], axis=1)

    b_arrived(0, b1)
    block[...] = b_part(0, 0)
    invert(block, block_high, block_low, x1)
    b_arrived(1, b2)
    x1_halves = split(x1[...])
    b12 = split(b_part(0, 1))
    t_halves = split(dot3(split(b_part(1, 0)), x1_halves))
    block[...] = b_part(1, 1) - dot3(t_halves, b12)
    own_c.wait()
    for which in range(4):
        c_swap(which)(me.col(-STEP[which - 1] if which else 0, 1)).wait_recv()
    lower = dot3(split(c_part(0)), x1_halves)
    l1[...] = lower
    lower = jnp.where(in1, 0.0, lower)
    c2[...] = c_part(1) - dot3(split(lower), b12)
    invert(block, block_high, block_low, x2)
    lower2 = dot3(split(c2[...]), split(x2[...]))
    l2[...] = lower2
    lower2 = jnp.where(in1 | in2, 0.0, lower2)
    halves = split(lower2)
    lt_high[:, 512:], lt_low[:, 512:] = halves
    lt_high[:, :512], lt_low[:, :512] = split(lower - dot3(halves, t_halves))

    own_u.wait()
    own_m.wait()
    for which in range(4):
        for index in range(3):
            for gather in (u1, u2):
                gather.arrive(which, index)
    for b in range(4):
        update = dot3((lt_high[...], lt_low[...]), split(ug[b].reshape(1024, 256)))
        col_tile = b * 8 + me.c
        new = m[:, b].reshape(512, 256) - update
        for j in range(4):
            window = slice(j % 2 * 256, j % 2 * 256 + 256)
            if j < 2:
                column = jnp.where(in1, cg[:, j].reshape(512, 256), l1[:, window])
            else:
                column = jnp.where(in1 | in2, c2[:, window], l2[:, window])
            new = jnp.where(col_tile == pivots[j], column, new)
        for half in range(2):
            out[pl.ds(2 * b + half, 512, stride=8), :] = new[:, half * 128 : half * 128 + 128]

    for index in range(15):
        row_spread(index)(me.r).wait_send()
    for index in range(7):
        col_spread(index)(me.c).wait_send()
        b_scatter(index)(me.c).wait_send()
        b_gather(index)(me.c).wait_send()
    for index in range(3):
        c_out(index)(me.c).wait_send()
    for which in range(4):
        c_swap(which)(me.c).wait_send()
    for gather in (u1, u2, b1, b2):
        gather.drain()
    for half in range(2):
        for slot in range(15):
            b_swap(half, slot, me.r, False).wait_send()


def eliminate(panel, m):
    plane = [DMA((3,)), DMA((3,)), DMA((12,)), DMA((12,))]
    square = pltpu.VMEM((512, 512), F32)
    narrow = pltpu.VMEM((512, 512), BF16)
    return pl.pallas_call(
        pivot_kernel,
        name="pivots",
        out_shape=jax.ShapeDtypeStruct((4096, 128), F32),
        in_specs=[SMEM, ANY],
        out_specs=VMEM,
        scratch_shapes=[
            pltpu.VMEM((2, 4, 256, 256), F32),
            pltpu.VMEM((16, 2, 4, 16, 256), F32),
            pltpu.VMEM((8, 4, 64, 256), F32),
            pltpu.VMEM((4, 4, 16, 16, 256), F32),
            pltpu.VMEM((4, 4, 16, 16, 256), F32),
            pltpu.VMEM((8, 4, 64, 256), F32),
            pltpu.VMEM((4, 4, 16, 256), F32),
            pltpu.VMEM((4, 64, 256), F32),
            pltpu.VMEM((8, 4, 8, 256), F32),
            pltpu.VMEM((4, 8, 256), F32),
            square, narrow, narrow, square, square, square, square, square,
            pltpu.VMEM((512, 1024), BF16), pltpu.VMEM((512, 1024), BF16),
            DMA((7,)),
            DMA((15,)), DMA((15,)), DMA((7,)), DMA((7,)),
            DMA((7,)), DMA((7,)), DMA((7,)), DMA((7,)),
            DMA((3,)), DMA((3,)), DMA((4,)), DMA((4,)),
            plane, plane, plane, plane,
            DMA((2, 15)), DMA((2, 15)),
        ],
        compiler_params=pltpu.CompilerParams(
            collective_id=1, has_side_effects=True, vmem_limit_bytes=56 * 2**20
        ),
    )(panel, m)


def shards(front_tiles, child_tiles, child_target, panel_tiles):
    targets = child_target.reshape(16, 2)
    spots = targets[:, 0] // 16 * 4 + targets[:, 1] // 8
    spots = jnp.broadcast_to(jnp.pad(spots, (0, 112)), (8, 128))
    tiles, landed = exchange_children(child_tiles.reshape(16, 256, 256), spots)
    m = extend_add(landed, front_tiles.reshape(4096, 128), tiles)
    return eliminate(panel_tiles, m).reshape(front_tiles.shape)


def solution(mesh):
    in_specs = (
        P(None, "row", None, None, "col", None),
        P("row", "col", None, None, None),
        P("row", "col", None, None),
        P(),
    )
    out_specs = P(None, "row", None, None, "col", None)
    return jax.shard_map(shards, mesh=mesh, in_specs=in_specs, out_specs=out_specs, check_vma=False)
```

```python
import jax
import jax.numpy as jnp
from jax import lax
from jax.experimental import pallas as pl
from jax.experimental.pallas import tpu as pltpu
from jax.sharding import PartitionSpec as P

MESH = pl.DeviceIdType.MESH
DMA = pltpu.SemaphoreType.DMA
ANY = pl.BlockSpec(memory_space=pl.ANY)
VMEM = pl.BlockSpec(memory_space=pltpu.VMEM)
SMEM = pl.BlockSpec(memory_space=pltpu.SMEM)
F32 = jnp.float32
BF16 = jnp.bfloat16

SQUARE = tuple((a, (a + s) % 4) for s in (1, 3, 0, 2) for a in (1, 3, 0, 2) if (a, s) != (0, 0))
PLANE = (
    (0, 1), (1, 0), (0, 3), (3, 0), (1, 1), (3, 3), (1, 3), (3, 1),
    (0, 2), (2, 0), (1, 2), (2, 1), (3, 2), (2, 3), (2, 2),
)
COLUMN = ((0, 1), (1, 0), (3, 0), (1, 1), (3, 1), (2, 0), (2, 1))
STEP = (1, 3, 2)
SHIFT = (0, -1, 1, 2)
WINDOW = 6
LOOSE_STEPS = 4
TIGHT_STEPS = 2


class Place:
    def __init__(self):
        self.r = lax.axis_index("row")
        self.c = lax.axis_index("col")
        self.z, self.x = self.r // 4, self.r % 4
        self.y, self.k = self.c // 2, self.c % 2

    def row(self, dz, dx):
        return (self.z + dz + 4) % 4 * 4 + (self.x + dx + 4) % 4

    def col(self, dy, dk):
        return (self.y + dy + 4) % 4 * 2 + (self.k + dk + 2) % 2


def remote(src, dst, send, recv, device):
    return pltpu.make_async_remote_copy(
        src_ref=src, dst_ref=dst, send_sem=send, recv_sem=recv, device_id=device, device_id_type=MESH
    )


def greet(me):
    barrier = pltpu.get_barrier_semaphore()
    for dz, dx in PLANE:
        pl.semaphore_signal(barrier, inc=1, device_id=(me.row(dz, dx), me.c), device_id_type=MESH)
    for dy, dk in COLUMN:
        pl.semaphore_signal(barrier, inc=1, device_id=(me.r, me.col(dy, dk)), device_id_type=MESH)
    pl.semaphore_wait(barrier, len(PLANE) + len(COLUMN))


class Children:
    def __init__(self, me, tiles, spots, mid, mid_spots, landed, landed_spots, sems):
        self.me, self.tiles, self.spots = me, tiles, spots
        self.mid, self.mid_spots, self.landed, self.landed_spots = mid, mid_spots, landed, landed_spots
        (
            self.own, self.own_spot, self.send1, self.recv1, self.spot_send1, self.spot_recv1,
            self.send2, self.recv2, self.spot_send2, self.spot_recv2,
        ) = sems

    def first(self, index):
        target = self.me.row(*SQUARE[index])
        device = (target, self.me.c)
        r = self.me.r
        return (
            remote(self.tiles.at[target], self.mid.at[r], self.send1.at[index], self.recv1.at[index], device),
            remote(
                self.spots, self.mid_spots.at[r], self.spot_send1.at[index], self.spot_recv1.at[index], device
            ),
        )

    def source(self, index):
        if index == len(SQUARE):
            return self.me.r, self.tiles.at[self.me.r], self.spots
        dz, dx = SQUARE[index]
        source = self.me.row(-dz, -dx)
        return source, self.mid.at[source], self.mid_spots.at[source]

    def _second(self, index, away):
        source, tile, spot = self.source(index)
        half = source // 8
        place = half * 8 + self.me.c
        if not away:
            return (
                pltpu.make_async_copy(tile, self.landed.at[place], self.own.at[half]),
                pltpu.make_async_copy(spot, self.landed_spots.at[place], self.own_spot.at[half]),
            )
        device = (self.me.r, source % 8)
        return (
            remote(tile, self.landed.at[place], self.send2.at[index], self.recv2.at[place], device),
            remote(
                spot, self.landed_spots.at[place], self.spot_send2.at[index], self.spot_recv2.at[place], device
            ),
        )

    def pass_on(self, index):
        if index < len(SQUARE):
            for copy in self.first(index):
                copy.wait_recv()
        col = self.source(index)[0] % 8

        @pl.when(col == self.me.c)
        def _():
            for copy in self._second(index, False):
                copy.start()

        @pl.when(col != self.me.c)
        def _():
            for copy in self._second(index, True):
                copy.start()

    def send(self):
        last = len(SQUARE)
        for index in range(last):
            if index == WINDOW:
                self.pass_on(last)
            if index >= WINDOW:
                self.pass_on(index - WINDOW)
            for copy in self.first(index):
                copy.start()
        for index in range(last - WINDOW, last):
            self.pass_on(index)

    def arrive(self, half, dy, dk):
        place = half * 8 + self.me.col(dy, dk)
        tile, spot = self.landed.at[place], self.landed_spots.at[place]
        if (dy, dk) == (0, 0):
            pltpu.make_async_copy(tile, tile, self.own.at[half]).wait()
            pltpu.make_async_copy(spot, spot, self.own_spot.at[half]).wait()
        else:
            device = (self.me.r, self.me.c)
            remote(tile, tile, self.send2.at[0], self.recv2.at[place], device).wait_recv()
            remote(spot, spot, self.spot_send2.at[0], self.spot_recv2.at[place], device).wait_recv()
        return place

    def drain(self):
        for index in range(len(SQUARE) + 1):
            if index < len(SQUARE):
                for copy in self.first(index):
                    copy.wait_send()
            col = self.source(index)[0] % 8

            @pl.when(col != self.me.c)
            def _(index=index):
                for copy in self._second(index, True):
                    copy.wait_send()


class PlaneGather:
    def __init__(self, me, at, own, x_first, relayed, sems):
        self.me, self.at, self.own, self.x_first = me, at, own, x_first
        self.send1, self.recv1, self.send2, self.recv2 = sems
        self.relayed = relayed
        self.near = range(2 if relayed else 3)
        self.far = (2, 3) if relayed else (2,)

    def number(self, one, two):
        return self.me.row(two, one) if self.x_first else self.me.row(one, two)

    def _copy(self, index, own, source, landed, send, recv, targets):
        block, landed = self.at(source) if own is None else own, self.at(landed)
        if self.relayed and index >= 2:
            half = pl.ds(2 * (index - 2), 2)
            block, landed = self.at(source).at[half], landed.at[half]
            index -= 2
        return remote(block, landed, send, recv, (targets[index], self.me.c))

    def _first(self, index, source, landed):
        targets = [self.number(step, 0) for step in (1, -1, 2)]
        return self._copy(
            index, self.own, source, landed, self.send1.at[index], self.recv1.at[index], targets
        )

    def _second(self, which, index, source, landed):
        targets = [self.number(0, step) for step in (1, -1, 2)]
        slot = which * 4 + index
        return self._copy(
            index, None if which else self.own, source, landed,
            self.send2.at[slot], self.recv2.at[slot], targets,
        )

    def start(self):
        for index in self.near:
            self._first(index, self.me.r, self.me.r).start()

    def relay(self):
        for index, shift in enumerate((-1, 1)):
            source = self.number(shift, 0)
            self._first(index, self.me.r, source).wait_recv()
            if self.relayed:
                self._first(index + 2, source, source).start()

    def forward(self, which):
        source = self.number(SHIFT[which], 0)
        if which == 3:
            for index in self.far:
                self._first(index, source, source).wait_recv()
        for index in self.near:
            self._second(which, index, source, source).start()
        return source

    def relay_second(self, which):
        landed = []
        for index, shift in enumerate((-1, 1)):
            source = self.number(SHIFT[which], shift)
            self._second(which, index, source, source).wait_recv()
            if self.relayed:
                self._second(which, index + 2, source, source).start()
            landed.append(source)
        return landed

    def finish(self, which):
        source = self.number(SHIFT[which], 2)
        for index in self.far:
            self._second(which, index, source, source).wait_recv()
        return source

    def drain(self):
        messages = (*range(2), *self.far)
        for index in messages:
            self._first(index, self.me.r, self.me.r).wait_send()
        for which in range(4):
            for index in messages:
                self._second(which, index, self.me.r, self.me.r).wait_send()


def split(value):
    high = value.astype(BF16)
    return high, (value - high.astype(F32)).astype(BF16)


def dot1(a, b):
    return jnp.dot(a, b, preferred_element_type=F32)


def dot3(a, b):
    return dot1(a[0], b[0]) + (dot1(a[0], b[1]) + dot1(a[1], b[0]))


def invert(block, block_high, block_low, estimate):
    size = block.shape[0]
    diagonal = lax.broadcasted_iota(jnp.int32, (size, size), 0) == lax.broadcasted_iota(
        jnp.int32, (size, size), 1
    )
    value = block[...]
    high, low = split(value)
    block_high[...] = high
    block_low[...] = low
    weights = jnp.sum(jnp.where(diagonal, value, 0.0), axis=0, keepdims=True)
    estimate[...] = jnp.where(diagonal, 1.0 / weights, 0.0)

    def loose(step, carry):
        now = estimate[...]
        high = now.astype(BF16)
        product = dot1(block_high[...], high)
        estimate[...] = 2.0 * now - dot1(high, product.astype(BF16))
        return carry

    def tight(step, carry):
        now = estimate[...]
        halves = split(now)
        product = dot3((block_high[...], block_low[...]), halves)
        estimate[...] = 2.0 * now - dot3(halves, split(product))
        return carry

    lax.fori_loop(0, LOOSE_STEPS, loose, 0)
    lax.fori_loop(0, TIGHT_STEPS, tight, 0)


def pivot_kernel(
    panel, targets, front, tiles, out, mid, mid_spots, spots, landed, landed_spots, m, result, rows, cols, ug, bg, cg, upc, cpc, bsc, bpc,
    block, block_high, block_low, x1, x2, l1, l2, c2, lt_high, lt_low, own,
    row_s, row_r, col_s, col_r, bs_s, bs_r, bc_s, bc_r, c_s, c_r, cx_s, cx_r, ua, ub, ba, bb, bx_s, bx_r,
    out_sem, child_sems,
):
    me = Place()
    greet(me)
    pivots = [panel[j // 2, j % 2] for j in range(4)]

    spots[...] = jnp.zeros_like(spots)
    spots[0:1, 0:16] = targets[0:1, :] // 16 * 4 + targets[1:2, :] // 8
    children = Children(me, tiles, spots, mid, mid_spots, landed, landed_spots, child_sems)
    children.send()
    for chunk in range(8):
        part = front[pl.ds(chunk, 512, stride=8), :].reshape(2, 256, 128)
        m[:, chunk // 2, :, pl.ds(chunk % 2 * 128, 128)] = part
    lane = lax.broadcasted_iota(jnp.int32, (8, 128), 1)
    for half in range(2):
        for dy, dk in ((0, 0), *COLUMN):
            place = children.arrive(half, dy, dk)
            spot = jnp.where(lane == me.r, landed_spots[place], 0)
            spot = jnp.sum(spot.astype(F32), keepdims=True).astype(jnp.int32)

            def add(slot, carry, place=place, spot=spot):
                m[slot // 4, slot % 4] += jnp.where(spot == slot, landed[place], 0.0)
                return carry

            lax.fori_loop(0, 8, add, 0)

    def row_slice(target):
        return m.at[:, :, pl.ds(pl.multiple_of(target * 16, 16), 16), :]

    def col_slice(target):
        return m.at[target // 4, :, pl.ds(pl.multiple_of(target % 4 * 64, 64), 64), :]

    def row_spread(index):
        target = me.row(*PLANE[index])
        return lambda source: remote(
            row_slice(target), rows.at[source], row_s.at[index], row_r.at[index], (target, me.c)
        )

    def col_spread(index):
        target = me.col(*COLUMN[index])
        return lambda source: remote(
            col_slice(target), cols.at[source], col_s.at[index], col_r.at[index], (me.r, target)
        )

    for index in range(15):
        row_spread(index)(me.r).start()
        if index < 7:
            col_spread(index)(me.c).start()
    mine = (
        pltpu.make_async_copy(row_slice(me.r), rows.at[me.r], own.at[0]),
        pltpu.make_async_copy(col_slice(me.c), cols.at[me.c], own.at[1]),
    )
    for copy in mine:
        copy.start()
    for copy in mine:
        copy.wait()
    for index, (dz, dx) in enumerate(PLANE):
        row_spread(index)(me.row(-dz, -dx)).wait_recv()
    for j, pivot in enumerate(pivots):
        upc[:, j] = rows[pivot % 16, pivot // 16]

    def b_rows(col):
        return upc.at[:, col // 2, pl.ds(pl.multiple_of(col % 2 * 8, 8), 8), :]

    def b_scatter(index):
        target = me.col(*COLUMN[index])
        return lambda source: remote(
            b_rows(target), bsc.at[source], bs_s.at[index], bs_r.at[index], (me.r, target)
        )

    for index in range(7):
        b_scatter(index)(me.c).start()
    own_scatter = pltpu.make_async_copy(b_rows(me.c), bsc.at[me.c], own.at[2])
    own_scatter.start()

    def u_at(first):
        return lambda source: ug.at[:, pl.ds(first, 2), source]

    u1 = PlaneGather(me, u_at(0), upc.at[:, pl.ds(0, 2)], True, True, ua)
    u2 = PlaneGather(me, u_at(2), upc.at[:, pl.ds(2, 2)], False, True, ub)
    u1.start()
    u2.start()
    own_u = pltpu.make_async_copy(upc, ug.at[:, :, me.r], own.at[3])
    own_u.start()

    own_scatter.wait()
    for index, (dy, dk) in enumerate(COLUMN):
        b_scatter(index)(me.col(-dy, -dk)).wait_recv()
    for j, pivot in enumerate(pivots):
        bpc[j] = bsc[pivot % 8, pivot // 8]

    def b_piece(col):
        return bg.at[:, col // 2, me.r, pl.ds(pl.multiple_of(col % 2 * 8, 8), 8), :]

    def b_gather(index):
        return lambda source: remote(
            bpc, b_piece(source), bc_s.at[index], bc_r.at[index], (me.r, me.col(*COLUMN[index]))
        )

    for index in range(7):
        b_gather(index)(me.c).start()
    own_b = pltpu.make_async_copy(bpc, b_piece(me.c), own.at[4])
    own_b.start()

    for index, (dy, dk) in enumerate(COLUMN):
        col_spread(index)(me.col(-dy, -dk)).wait_recv()
    for j, pivot in enumerate(pivots):
        cpc[j] = cols[pivot % 8, pivot // 8]

    def c_out(index):
        return lambda source: remote(
            cpc, cg.at[source], c_s.at[index], c_r.at[index], (me.r, me.col(STEP[index], 0))
        )

    def c_swap(which):
        source = me.col(-STEP[which - 1] if which else 0, 0)
        src = cg.at[source] if which else cpc
        return lambda landed: remote(
            src, cg.at[landed], cx_s.at[which], cx_r.at[which], (me.r, me.col(0, 1))
        )

    own_b.wait()
    for index, (dy, dk) in enumerate(COLUMN):
        b_gather(index)(me.col(-dy, -dk)).wait_recv()

    def b_at(pivot):
        return lambda source: bg.at[:, pivot, source]

    b1 = PlaneGather(me, b_at(me.k), b_at(me.k)(me.r), True, False, ba)
    b2 = PlaneGather(me, b_at(2 + me.k), b_at(2 + me.k)(me.r), False, False, bb)
    b1.start()
    b2.start()

    def b_swap(half, slot, source, back):
        pivot = 2 * half + (1 - me.k if back else me.k)
        block = bg.at[:, pivot, source]
        return remote(block, block, bx_s.at[half, slot], bx_r.at[half, slot], (me.r, me.col(0, 1)))

    for gather in (b1, b2):
        gather.forward(0)
    for index in range(3):
        c_out(index)(me.c).start()
    c_swap(0)(me.c).start()
    own_c = pltpu.make_async_copy(cpc, cg.at[me.c], own.at[5])
    own_c.start()

    for gather in (u1, u2, b1, b2):
        gather.relay()
    for which in range(1, 4):
        for half, gather in enumerate((b1, b2)):
            source = gather.forward(which)
            b_swap(half, which - 1, source, False).start()
    for which in range(4):
        for gather in (u1, u2):
            gather.forward(which)
    for which in range(4):
        for half, gather in enumerate((b1, b2)):
            for index, source in enumerate(gather.relay_second(which)):
                b_swap(half, 3 + which * 3 + index, source, False).start()
    for which in range(1, 4):
        source = me.col(-STEP[which - 1], 0)
        c_out(which - 1)(source).wait_recv()
        c_swap(which)(source).start()
    for gather in (u1, u2):
        gather.relay_second(0)
    for half, gather in enumerate((b1, b2)):
        for which in range(4):
            source = gather.finish(which)
            b_swap(half, 5 + which * 3, source, False).start()

    def b_arrived(half, gather):
        for which in range(4):
            if which:
                source = gather.number(SHIFT[which], 0)
                b_swap(half, which - 1, source, True).wait_recv()
            for index, shift in enumerate((-1, 1, 2)):
                source = gather.number(SHIFT[which], shift)
                b_swap(half, 3 + which * 3 + index, source, True).wait_recv()

    def u_relay(which):
        for gather in (u1, u2):
            gather.relay_second(which)

    row_tile = (lax.broadcasted_iota(jnp.int32, (512, 1), 0) // 256) * 16 + me.r
    in1 = (row_tile == pivots[0]) | (row_tile == pivots[1])
    in2 = (row_tile == pivots[2]) | (row_tile == pivots[3])

    def b_part(rows, cols):
        return jnp.concatenate(
            [bg[2 * cols + j, pl.ds(2 * rows, 2)].reshape(512, 256) for j in range(2)], axis=1
        )

    def c_part(cols):
        return jnp.concatenate([cg[:, 2 * cols + j].reshape(512, 256) for j in range(2)], axis=1)

    b_arrived(0, b1)
    block[...] = b_part(0, 0)
    u_relay(1)
    invert(block, block_high, block_low, x1)
    b_arrived(1, b2)
    u_relay(2)
    x1_halves = split(x1[...])
    b12 = split(b_part(0, 1))
    t_halves = split(dot3(split(b_part(1, 0)), x1_halves))
    block[...] = b_part(1, 1) - dot3(t_halves, b12)
    u_relay(3)
    own_c.wait()
    for which in range(4):
        c_swap(which)(me.col(-STEP[which - 1] if which else 0, 1)).wait_recv()
    lower = dot3(split(c_part(0)), x1_halves)
    l1[...] = lower
    lower = jnp.where(in1, 0.0, lower)
    c2[...] = c_part(1) - dot3(split(lower), b12)
    invert(block, block_high, block_low, x2)
    lower2 = dot3(split(c2[...]), split(x2[...]))
    l2[...] = lower2
    lower2 = jnp.where(in1 | in2, 0.0, lower2)
    halves = split(lower2)
    lt_high[:, 512:], lt_low[:, 512:] = halves
    lt_high[:, :512], lt_low[:, :512] = split(lower - dot3(halves, t_halves))

    own_u.wait()
    for which in range(4):
        for gather in (u1, u2):
            gather.finish(which)
    for b in range(4):
        update = dot3((lt_high[...], lt_low[...]), split(ug[b].reshape(1024, 256)))
        col_tile = b * 8 + me.c
        new = m[:, b].reshape(512, 256) - update
        for j in range(4):
            window = slice(j % 2 * 256, j % 2 * 256 + 256)
            if j < 2:
                column = jnp.where(in1, cg[:, j].reshape(512, 256), l1[:, window])
            else:
                column = jnp.where(in1 | in2, c2[:, window], l2[:, window])
            new = jnp.where(col_tile == pivots[j], column, new)
        for half in range(2):
            result[pl.ds(2 * b + half, 512, stride=8), :] = new[:, half * 128 : half * 128 + 128]

    written = [
        pltpu.make_async_copy(result.at[pl.ds(512 * i, 512)], out.at[pl.ds(512 * i, 512)], out_sem.at[i])
        for i in range(8)
    ]
    for copy in written:
        copy.start()
    children.drain()
    for index in range(15):
        row_spread(index)(me.r).wait_send()
    for index in range(7):
        col_spread(index)(me.c).wait_send()
        b_scatter(index)(me.c).wait_send()
        b_gather(index)(me.c).wait_send()
    for index in range(3):
        c_out(index)(me.c).wait_send()
    for which in range(4):
        c_swap(which)(me.c).wait_send()
    for gather in (u1, u2, b1, b2):
        gather.drain()
    for half in range(2):
        for slot in range(15):
            b_swap(half, slot, me.r, False).wait_send()
    for copy in written:
        copy.wait()


def eliminate(panel, targets, front, tiles):
    plane = [DMA((4,)), DMA((4,)), DMA((16,)), DMA((16,))]
    square = pltpu.VMEM((512, 512), F32)
    narrow = pltpu.VMEM((512, 512), BF16)
    return pl.pallas_call(
        pivot_kernel,
        name="pivots",
        out_shape=[
            jax.ShapeDtypeStruct((4096, 128), F32),
            jax.ShapeDtypeStruct((16, 256, 256), F32),
            jax.ShapeDtypeStruct((16, 8, 128), jnp.int32),
        ],
        in_specs=[SMEM, VMEM, VMEM, ANY],
        out_specs=[ANY] * 3,
        scratch_shapes=[
            pltpu.VMEM((8, 128), jnp.int32),
            pltpu.VMEM((16, 256, 256), F32),
            pltpu.VMEM((16, 8, 128), jnp.int32),
            pltpu.VMEM((2, 4, 256, 256), F32),
            pltpu.VMEM((4096, 128), F32),
            pltpu.VMEM((16, 2, 4, 16, 256), F32),
            pltpu.VMEM((8, 4, 64, 256), F32),
            pltpu.VMEM((4, 4, 16, 16, 256), F32),
            pltpu.VMEM((4, 4, 16, 16, 256), F32),
            pltpu.VMEM((8, 4, 64, 256), F32),
            pltpu.VMEM((4, 4, 16, 256), F32),
            pltpu.VMEM((4, 64, 256), F32),
            pltpu.VMEM((8, 4, 8, 256), F32),
            pltpu.VMEM((4, 8, 256), F32),
            square, narrow, narrow, square, square, square, square, square,
            pltpu.VMEM((512, 1024), BF16), pltpu.VMEM((512, 1024), BF16),
            DMA((7,)),
            DMA((15,)), DMA((15,)), DMA((7,)), DMA((7,)),
            DMA((7,)), DMA((7,)), DMA((7,)), DMA((7,)),
            DMA((3,)), DMA((3,)), DMA((4,)), DMA((4,)),
            plane, plane, plane, plane,
            DMA((2, 15)), DMA((2, 15)),
            DMA((8,)), [DMA((2,)), DMA((2,))] + [DMA((16,))] * 8,
        ],
        compiler_params=pltpu.CompilerParams(
            collective_id=0, has_side_effects=True, vmem_limit_bytes=56 * 2**20
        ),
    )(panel, targets, front, tiles)[0]


def hand_over_kernel(source, out, sems):
    copies = [
        pltpu.make_async_copy(source.at[pl.ds(512 * i, 512)], out.at[pl.ds(512 * i, 512)], sems.at[i])
        for i in range(8)
    ]
    for copy in copies:
        copy.start()
    for copy in copies:
        copy.wait()


def hand_over(result):
    return pl.pallas_call(
        hand_over_kernel,
        name="hand_over",
        out_shape=jax.ShapeDtypeStruct(result.shape, result.dtype),
        in_specs=[VMEM],
        out_specs=ANY,
        scratch_shapes=[DMA((8,))],
    )(result)


def shards(front_tiles, child_tiles, child_target, panel_tiles):
    result = eliminate(
        panel_tiles,
        child_target.reshape(16, 2).T,
        front_tiles.reshape(4096, 128),
        child_tiles.reshape(16, 256, 256),
    )
    return hand_over(result).reshape(front_tiles.shape)


def solution(mesh):
    in_specs = (
        P(None, "row", None, None, "col", None),
        P("row", "col", None, None, None),
        P("row", "col", None, None),
        P(),
    )
    out_specs = P(None, "row", None, None, "col", None)
    return jax.shard_map(shards, mesh=mesh, in_specs=in_specs, out_specs=out_specs, check_vma=False)
```

```python
import jax
import jax.numpy as jnp
from jax import lax
from jax.experimental import pallas as pl
from jax.experimental.pallas import tpu as pltpu
from jax.sharding import PartitionSpec as P

MESH = pl.DeviceIdType.MESH
DMA = pltpu.SemaphoreType.DMA
ANY = pl.BlockSpec(memory_space=pl.ANY)
VMEM = pl.BlockSpec(memory_space=pltpu.VMEM)
SMEM = pl.BlockSpec(memory_space=pltpu.SMEM)
F32 = jnp.float32
BF16 = jnp.bfloat16

SQUARE = tuple((a, (a + s) % 4) for s in (1, 3, 0, 2) for a in (1, 3, 0, 2) if (a, s) != (0, 0))
PLANE = (
    (0, 1), (1, 0), (0, 3), (3, 0), (1, 1), (3, 3), (1, 3), (3, 1),
    (0, 2), (2, 0), (1, 2), (2, 1), (3, 2), (2, 3), (2, 2),
)
COLUMN = ((0, 1), (1, 0), (3, 0), (1, 1), (3, 1), (2, 0), (2, 1))
STEP = (1, 3, 2)
SHIFT = (0, -1, 1, 2)
WINDOW = 6
LOOSE_STEPS = 3


class Place:
    def __init__(self):
        self.r = lax.axis_index("row")
        self.c = lax.axis_index("col")
        self.z, self.x = self.r // 4, self.r % 4
        self.y, self.k = self.c // 2, self.c % 2

    def row(self, dz, dx):
        return (self.z + dz + 4) % 4 * 4 + (self.x + dx + 4) % 4

    def col(self, dy, dk):
        return (self.y + dy + 4) % 4 * 2 + (self.k + dk + 2) % 2


def remote(src, dst, send, recv, device):
    return pltpu.make_async_remote_copy(
        src_ref=src, dst_ref=dst, send_sem=send, recv_sem=recv, device_id=device, device_id_type=MESH
    )


def greet(me):
    barrier = pltpu.get_barrier_semaphore()
    for dz, dx in PLANE:
        pl.semaphore_signal(barrier, inc=1, device_id=(me.row(dz, dx), me.c), device_id_type=MESH)
    for dy, dk in COLUMN:
        pl.semaphore_signal(barrier, inc=1, device_id=(me.r, me.col(dy, dk)), device_id_type=MESH)
    pl.semaphore_wait(barrier, len(PLANE) + len(COLUMN))


class Children:
    def __init__(self, me, tiles, spots, mid, mid_spots, landed, landed_spots, sems):
        self.me, self.tiles, self.spots = me, tiles, spots
        self.mid, self.mid_spots, self.landed, self.landed_spots = mid, mid_spots, landed, landed_spots
        (
            self.own, self.own_spot, self.send1, self.recv1, self.spot_send1, self.spot_recv1,
            self.send2, self.recv2, self.spot_send2, self.spot_recv2,
        ) = sems

    def first(self, index):
        target = self.me.row(*SQUARE[index])
        device = (target, self.me.c)
        r = self.me.r
        return (
            remote(self.tiles.at[target], self.mid.at[r], self.send1.at[index], self.recv1.at[index], device),
            remote(
                self.spots, self.mid_spots.at[r], self.spot_send1.at[index], self.spot_recv1.at[index], device
            ),
        )

    def source(self, index):
        if index == len(SQUARE):
            return self.me.r, self.tiles.at[self.me.r], self.spots
        dz, dx = SQUARE[index]
        source = self.me.row(-dz, -dx)
        return source, self.mid.at[source], self.mid_spots.at[source]

    def _second(self, index, away):
        source, tile, spot = self.source(index)
        half = source // 8
        place = half * 8 + self.me.c
        if not away:
            return (
                pltpu.make_async_copy(tile, self.landed.at[place], self.own.at[half]),
                pltpu.make_async_copy(spot, self.landed_spots.at[place], self.own_spot.at[half]),
            )
        device = (self.me.r, source % 8)
        return (
            remote(tile, self.landed.at[place], self.send2.at[index], self.recv2.at[place], device),
            remote(
                spot, self.landed_spots.at[place], self.spot_send2.at[index], self.spot_recv2.at[place], device
            ),
        )

    def pass_on(self, index):
        if index < len(SQUARE):
            for copy in self.first(index):
                copy.wait_recv()
        col = self.source(index)[0] % 8

        @pl.when(col == self.me.c)
        def _():
            for copy in self._second(index, False):
                copy.start()

        @pl.when(col != self.me.c)
        def _():
            for copy in self._second(index, True):
                copy.start()

    def send(self):
        last = len(SQUARE)
        for index in range(last):
            if index == WINDOW:
                self.pass_on(last)
            if index >= WINDOW:
                self.pass_on(index - WINDOW)
            for copy in self.first(index):
                copy.start()
        for index in range(last - WINDOW, last):
            self.pass_on(index)

    def first_half(self):
        def rank(value):
            return jnp.where(value == 1, 0, jnp.where(value == 3, 1, jnp.where(value == 0, 2, 3)))

        steps = []
        for half in range(2):
            source = self.me.c + 8 * half
            dz, dx = (self.me.z - source // 4 + 4) % 4, (self.me.x - source % 4 + 4) % 4
            step = 4 * rank((dx - dz + 4) % 4) + rank(dz)
            steps.append(jnp.where(source == self.me.r, -1, step))
        return jnp.where(steps[0] < steps[1], 0, 1)

    def arrive(self, half, dy, dk):
        place = half * 8 + self.me.col(dy, dk)
        tile, spot = self.landed.at[place], self.landed_spots.at[place]
        if (dy, dk) == (0, 0):
            pltpu.make_async_copy(tile, tile, self.own.at[half]).wait()
            pltpu.make_async_copy(spot, spot, self.own_spot.at[half]).wait()
        else:
            device = (self.me.r, self.me.c)
            remote(tile, tile, self.send2.at[0], self.recv2.at[place], device).wait_recv()
            remote(spot, spot, self.spot_send2.at[0], self.spot_recv2.at[place], device).wait_recv()
        return place

    def drain(self):
        for index in range(len(SQUARE) + 1):
            if index < len(SQUARE):
                for copy in self.first(index):
                    copy.wait_send()
            col = self.source(index)[0] % 8

            @pl.when(col != self.me.c)
            def _(index=index):
                for copy in self._second(index, True):
                    copy.wait_send()


class PlaneGather:
    def __init__(self, me, at, own, x_first, relayed, sems):
        self.me, self.at, self.own, self.x_first = me, at, own, x_first
        self.send1, self.recv1, self.send2, self.recv2 = sems
        self.relayed = relayed
        self.near = range(2 if relayed else 3)
        self.far = (2, 3) if relayed else (2,)

    def number(self, one, two):
        return self.me.row(two, one) if self.x_first else self.me.row(one, two)

    def _copy(self, index, own, source, landed, send, recv, targets):
        block, landed = self.at(source) if own is None else own, self.at(landed)
        if self.relayed and index >= 2:
            half = pl.ds(2 * (index - 2), 2)
            block, landed = self.at(source).at[half], landed.at[half]
            index -= 2
        return remote(block, landed, send, recv, (targets[index], self.me.c))

    def _first(self, index, source, landed):
        targets = [self.number(step, 0) for step in (1, -1, 2)]
        return self._copy(
            index, self.own, source, landed, self.send1.at[index], self.recv1.at[index], targets
        )

    def _second(self, which, index, source, landed):
        targets = [self.number(0, step) for step in (1, -1, 2)]
        slot = which * 4 + index
        return self._copy(
            index, None if which else self.own, source, landed,
            self.send2.at[slot], self.recv2.at[slot], targets,
        )

    def start(self):
        for index in self.near:
            self._first(index, self.me.r, self.me.r).start()

    def relay(self):
        for index, shift in enumerate((-1, 1)):
            source = self.number(shift, 0)
            self._first(index, self.me.r, source).wait_recv()
            if self.relayed:
                self._first(index + 2, source, source).start()

    def forward(self, which):
        source = self.number(SHIFT[which], 0)
        if which == 3:
            for index in self.far:
                self._first(index, source, source).wait_recv()
        for index in self.near:
            self._second(which, index, source, source).start()
        return source

    def relay_second(self, which):
        landed = []
        for index, shift in enumerate((-1, 1)):
            source = self.number(SHIFT[which], shift)
            self._second(which, index, source, source).wait_recv()
            if self.relayed:
                self._second(which, index + 2, source, source).start()
            landed.append(source)
        return landed

    def finish(self, which):
        source = self.number(SHIFT[which], 2)
        for index in self.far:
            self._second(which, index, source, source).wait_recv()
        return source

    def drain(self):
        messages = (*range(2), *self.far)
        for index in messages:
            self._first(index, self.me.r, self.me.r).wait_send()
        for which in range(4):
            for index in messages:
                self._second(which, index, self.me.r, self.me.r).wait_send()


def split(value):
    high = value.astype(BF16)
    return high, (value - high.astype(F32)).astype(BF16)


def dot1(a, b):
    return jnp.dot(a, b, preferred_element_type=F32)


def dot3(a, b):
    return dot1(a[0], b[0]) + (dot1(a[0], b[1]) + dot1(a[1], b[0]))


def invert(block, block_high, block_low, estimate):
    size = block.shape[0]
    diagonal = lax.broadcasted_iota(jnp.int32, (size, size), 0) == lax.broadcasted_iota(
        jnp.int32, (size, size), 1
    )
    value = block[...]
    block_high[...], block_low[...] = split(value)
    weights = jnp.where(diagonal, value, 0.0)
    by_row = 1.0 / jnp.sum(weights, axis=1, keepdims=True)
    by_col = 1.0 / jnp.sum(weights, axis=0, keepdims=True)
    estimate[...] = jnp.where(diagonal, by_col, -(by_row * value * by_col))

    def loose(step, carry):
        now = estimate[...]
        high = now.astype(BF16)
        product = dot1(block_high[...], high)
        estimate[...] = 2.0 * now - dot1(high, product.astype(BF16))
        return carry

    def residual(halves):
        return jnp.where(diagonal, 1.0, 0.0) - dot3((block_high[...], block_low[...]), halves)

    lax.fori_loop(0, LOOSE_STEPS, loose, 0)
    now = estimate[...]
    halves = split(now)
    estimate[...] = now + dot1(halves[0], residual(halves).astype(BF16))
    now = estimate[...]
    halves = split(now)
    estimate[...] = now + dot3(halves, split(residual(halves)))


def pivot_kernel(
    panel, targets, front, tiles, out, mid, mid_spots, spots, landed, landed_spots, m, result, rows, cols, ug, bg, cg, upc, cpc, bsc, bpc,
    block, block_high, block_low, x1, x2, l1, l2, c2, lt_high, lt_low, own,
    row_s, row_r, col_s, col_r, bs_s, bs_r, bc_s, bc_r, c_s, c_r, cx_s, cx_r, ua, ub, ba, bb, bx_s, bx_r,
    out_sem, child_sems,
):
    me = Place()
    greet(me)
    pivots = [panel[j // 2, j % 2] for j in range(4)]

    spots[...] = jnp.zeros_like(spots)
    spots[0:1, 0:16] = targets[0:1, :] // 16 * 4 + targets[1:2, :] // 8
    children = Children(me, tiles, spots, mid, mid_spots, landed, landed_spots, child_sems)
    children.send()
    for chunk in range(8):
        part = front[pl.ds(chunk, 512, stride=8), :].reshape(2, 256, 128)
        m[:, chunk // 2, :, pl.ds(chunk % 2 * 128, 128)] = part
    lane = lax.broadcasted_iota(jnp.int32, (8, 128), 1)
    first_half = children.first_half()
    for half in (first_half, 1 - first_half):
        for group in (((0, 0), *COLUMN[:3]), COLUMN[3:]):
            places = [children.arrive(half, dy, dk) for dy, dk in group]
            spot = []
            for place in places:
                mine = jnp.where(lane == me.r, landed_spots[place], 0)
                spot.append(jnp.sum(mine.astype(F32), keepdims=True).astype(jnp.int32))

            def add(slot, carry, places=places, spot=spot):
                parts = [jnp.where(s == slot, landed[p], 0.0) for s, p in zip(spot, places)]
                m[slot // 4, slot % 4] += (parts[0] + parts[1]) + (parts[2] + parts[3])
                return carry

            lax.fori_loop(0, 8, add, 0)

    def row_slice(target):
        return m.at[:, :, pl.ds(pl.multiple_of(target * 16, 16), 16), :]

    def col_slice(target):
        return m.at[target // 4, :, pl.ds(pl.multiple_of(target % 4 * 64, 64), 64), :]

    def row_spread(index):
        target = me.row(*PLANE[index])
        return lambda source: remote(
            row_slice(target), rows.at[source], row_s.at[index], row_r.at[index], (target, me.c)
        )

    def col_spread(index):
        target = me.col(*COLUMN[index])
        return lambda source: remote(
            col_slice(target), cols.at[source], col_s.at[index], col_r.at[index], (me.r, target)
        )

    for index in range(15):
        row_spread(index)(me.r).start()
        if index < 7:
            col_spread(index)(me.c).start()
    mine = (
        pltpu.make_async_copy(row_slice(me.r), rows.at[me.r], own.at[0]),
        pltpu.make_async_copy(col_slice(me.c), cols.at[me.c], own.at[1]),
    )
    for copy in mine:
        copy.start()
    for copy in mine:
        copy.wait()
    for index, (dz, dx) in enumerate(PLANE):
        row_spread(index)(me.row(-dz, -dx)).wait_recv()
    for j, pivot in enumerate(pivots):
        upc[:, j] = rows[pivot % 16, pivot // 16]

    def b_rows(col):
        return upc.at[:, col // 2, pl.ds(pl.multiple_of(col % 2 * 8, 8), 8), :]

    def b_scatter(index):
        target = me.col(*COLUMN[index])
        return lambda source: remote(
            b_rows(target), bsc.at[source], bs_s.at[index], bs_r.at[index], (me.r, target)
        )

    for index in range(7):
        b_scatter(index)(me.c).start()
    own_scatter = pltpu.make_async_copy(b_rows(me.c), bsc.at[me.c], own.at[2])
    own_scatter.start()

    def u_at(first):
        return lambda source: ug.at[:, pl.ds(first, 2), source]

    u1 = PlaneGather(me, u_at(0), upc.at[:, pl.ds(0, 2)], True, True, ua)
    u2 = PlaneGather(me, u_at(2), upc.at[:, pl.ds(2, 2)], False, True, ub)
    u1.start()
    u2.start()
    own_u = pltpu.make_async_copy(upc, ug.at[:, :, me.r], own.at[3])
    own_u.start()

    own_scatter.wait()
    for index, (dy, dk) in enumerate(COLUMN):
        b_scatter(index)(me.col(-dy, -dk)).wait_recv()
    for j, pivot in enumerate(pivots):
        bpc[j] = bsc[pivot % 8, pivot // 8]

    def b_piece(col):
        return bg.at[:, col // 2, me.r, pl.ds(pl.multiple_of(col % 2 * 8, 8), 8), :]

    def b_gather(index):
        return lambda source: remote(
            bpc, b_piece(source), bc_s.at[index], bc_r.at[index], (me.r, me.col(*COLUMN[index]))
        )

    for index in range(7):
        b_gather(index)(me.c).start()
    own_b = pltpu.make_async_copy(bpc, b_piece(me.c), own.at[4])
    own_b.start()

    for index, (dy, dk) in enumerate(COLUMN):
        col_spread(index)(me.col(-dy, -dk)).wait_recv()
    for j, pivot in enumerate(pivots):
        cpc[j] = cols[pivot % 8, pivot // 8]

    def c_out(index):
        return lambda source: remote(
            cpc, cg.at[source], c_s.at[index], c_r.at[index], (me.r, me.col(STEP[index], 0))
        )

    def c_swap(which):
        source = me.col(-STEP[which - 1] if which else 0, 0)
        src = cg.at[source] if which else cpc
        return lambda landed: remote(
            src, cg.at[landed], cx_s.at[which], cx_r.at[which], (me.r, me.col(0, 1))
        )

    own_b.wait()
    for index, (dy, dk) in enumerate(COLUMN):
        b_gather(index)(me.col(-dy, -dk)).wait_recv()

    def b_at(pivot):
        return lambda source: bg.at[:, pivot, source]

    b1 = PlaneGather(me, b_at(me.k), b_at(me.k)(me.r), True, False, ba)
    b2 = PlaneGather(me, b_at(2 + me.k), b_at(2 + me.k)(me.r), False, False, bb)
    b1.start()
    b2.start()

    def b_swap(half, slot, source, back):
        pivot = 2 * half + (1 - me.k if back else me.k)
        block = bg.at[:, pivot, source]
        return remote(block, block, bx_s.at[half, slot], bx_r.at[half, slot], (me.r, me.col(0, 1)))

    for gather in (b1, b2):
        gather.forward(0)
    for index in range(3):
        c_out(index)(me.c).start()
    c_swap(0)(me.c).start()
    own_c = pltpu.make_async_copy(cpc, cg.at[me.c], own.at[5])
    own_c.start()

    for gather in (u1, u2, b1, b2):
        gather.relay()
    for which in range(1, 4):
        for half, gather in enumerate((b1, b2)):
            source = gather.forward(which)
            b_swap(half, which - 1, source, False).start()
    for which in range(4):
        for gather in (u1, u2):
            gather.forward(which)
    for which in range(4):
        for half, gather in enumerate((b1, b2)):
            for index, source in enumerate(gather.relay_second(which)):
                b_swap(half, 3 + which * 3 + index, source, False).start()
    for which in range(1, 4):
        source = me.col(-STEP[which - 1], 0)
        c_out(which - 1)(source).wait_recv()
        c_swap(which)(source).start()
    for gather in (u1, u2):
        gather.relay_second(0)
    for half, gather in enumerate((b1, b2)):
        for which in range(4):
            source = gather.finish(which)
            b_swap(half, 5 + which * 3, source, False).start()

    def b_arrived(half, gather):
        for which in range(4):
            if which:
                source = gather.number(SHIFT[which], 0)
                b_swap(half, which - 1, source, True).wait_recv()
            for index, shift in enumerate((-1, 1, 2)):
                source = gather.number(SHIFT[which], shift)
                b_swap(half, 3 + which * 3 + index, source, True).wait_recv()

    def u_relay(which):
        for gather in (u1, u2):
            gather.relay_second(which)

    row_tile = (lax.broadcasted_iota(jnp.int32, (512, 1), 0) // 256) * 16 + me.r
    in1 = (row_tile == pivots[0]) | (row_tile == pivots[1])
    in2 = (row_tile == pivots[2]) | (row_tile == pivots[3])

    def b_part(rows, cols):
        return jnp.concatenate(
            [bg[2 * cols + j, pl.ds(2 * rows, 2)].reshape(512, 256) for j in range(2)], axis=1
        )

    def c_part(cols):
        return jnp.concatenate([cg[:, 2 * cols + j].reshape(512, 256) for j in range(2)], axis=1)

    b_arrived(0, b1)
    block[...] = b_part(0, 0)
    u_relay(1)
    invert(block, block_high, block_low, x1)
    b_arrived(1, b2)
    u_relay(2)
    x1_halves = split(x1[...])
    b12 = split(b_part(0, 1))
    t_halves = split(dot3(split(b_part(1, 0)), x1_halves))
    block[...] = b_part(1, 1) - dot3(t_halves, b12)
    u_relay(3)
    own_c.wait()
    for which in range(4):
        c_swap(which)(me.col(-STEP[which - 1] if which else 0, 1)).wait_recv()
    lower = dot3(split(c_part(0)), x1_halves)
    l1[...] = lower
    lower = jnp.where(in1, 0.0, lower)
    c2[...] = c_part(1) - dot3(split(lower), b12)
    invert(block, block_high, block_low, x2)
    lower2 = dot3(split(c2[...]), split(x2[...]))
    l2[...] = lower2
    lower2 = jnp.where(in1 | in2, 0.0, lower2)
    halves = split(lower2)
    lt_high[:, 512:], lt_low[:, 512:] = halves
    lt_high[:, :512], lt_low[:, :512] = split(lower - dot3(halves, t_halves))

    own_u.wait()
    for which in range(4):
        for gather in (u1, u2):
            gather.finish(which)
    for b in range(4):
        update = dot3((lt_high[...], lt_low[...]), split(ug[b].reshape(1024, 256)))
        col_tile = b * 8 + me.c
        new = m[:, b].reshape(512, 256) - update
        for j in range(4):
            window = slice(j % 2 * 256, j % 2 * 256 + 256)
            if j < 2:
                column = jnp.where(in1, cg[:, j].reshape(512, 256), l1[:, window])
            else:
                column = jnp.where(in1 | in2, c2[:, window], l2[:, window])
            new = jnp.where(col_tile == pivots[j], column, new)
        for half in range(2):
            result[pl.ds(2 * b + half, 512, stride=8), :] = new[:, half * 128 : half * 128 + 128]

    written = [
        pltpu.make_async_copy(result.at[pl.ds(512 * i, 512)], out.at[pl.ds(512 * i, 512)], out_sem.at[i])
        for i in range(8)
    ]
    for copy in written:
        copy.start()
    children.drain()
    for index in range(15):
        row_spread(index)(me.r).wait_send()
    for index in range(7):
        col_spread(index)(me.c).wait_send()
        b_scatter(index)(me.c).wait_send()
        b_gather(index)(me.c).wait_send()
    for index in range(3):
        c_out(index)(me.c).wait_send()
    for which in range(4):
        c_swap(which)(me.c).wait_send()
    for gather in (u1, u2, b1, b2):
        gather.drain()
    for half in range(2):
        for slot in range(15):
            b_swap(half, slot, me.r, False).wait_send()
    for copy in written:
        copy.wait()


def eliminate(panel, targets, front, tiles):
    plane = [DMA((4,)), DMA((4,)), DMA((16,)), DMA((16,))]
    square = pltpu.VMEM((512, 512), F32)
    narrow = pltpu.VMEM((512, 512), BF16)
    return pl.pallas_call(
        pivot_kernel,
        name="pivots",
        out_shape=[
            jax.ShapeDtypeStruct((4096, 128), F32),
            jax.ShapeDtypeStruct((16, 256, 256), F32),
            jax.ShapeDtypeStruct((16, 8, 128), jnp.int32),
        ],
        in_specs=[SMEM, VMEM, VMEM, ANY],
        out_specs=[ANY] * 3,
        scratch_shapes=[
            pltpu.VMEM((8, 128), jnp.int32),
            pltpu.VMEM((16, 256, 256), F32),
            pltpu.VMEM((16, 8, 128), jnp.int32),
            pltpu.VMEM((2, 4, 256, 256), F32),
            pltpu.VMEM((4096, 128), F32),
            pltpu.VMEM((16, 2, 4, 16, 256), F32),
            pltpu.VMEM((8, 4, 64, 256), F32),
            pltpu.VMEM((4, 4, 16, 16, 256), F32),
            pltpu.VMEM((4, 4, 16, 16, 256), F32),
            pltpu.VMEM((8, 4, 64, 256), F32),
            pltpu.VMEM((4, 4, 16, 256), F32),
            pltpu.VMEM((4, 64, 256), F32),
            pltpu.VMEM((8, 4, 8, 256), F32),
            pltpu.VMEM((4, 8, 256), F32),
            square, narrow, narrow, square, square, square, square, square,
            pltpu.VMEM((512, 1024), BF16), pltpu.VMEM((512, 1024), BF16),
            DMA((7,)),
            DMA((15,)), DMA((15,)), DMA((7,)), DMA((7,)),
            DMA((7,)), DMA((7,)), DMA((7,)), DMA((7,)),
            DMA((3,)), DMA((3,)), DMA((4,)), DMA((4,)),
            plane, plane, plane, plane,
            DMA((2, 15)), DMA((2, 15)),
            DMA((8,)), [DMA((2,)), DMA((2,))] + [DMA((16,))] * 8,
        ],
        compiler_params=pltpu.CompilerParams(
            collective_id=0, has_side_effects=True, vmem_limit_bytes=44 * 2**20
        ),
    )(panel, targets, front, tiles)[0]


def hand_over_kernel(source, out, sems):
    copies = [
        pltpu.make_async_copy(source.at[pl.ds(512 * i, 512)], out.at[pl.ds(512 * i, 512)], sems.at[i])
        for i in range(8)
    ]
    for copy in copies:
        copy.start()
    for copy in copies:
        copy.wait()


def hand_over(result):
    return pl.pallas_call(
        hand_over_kernel,
        name="hand_over",
        out_shape=jax.ShapeDtypeStruct(result.shape, result.dtype),
        in_specs=[VMEM],
        out_specs=ANY,
        scratch_shapes=[DMA((8,))],
    )(result)


def shards(front_tiles, child_tiles, child_target, panel_tiles):
    result = eliminate(
        panel_tiles,
        child_target.reshape(16, 2).T,
        front_tiles.reshape(4096, 128),
        child_tiles.reshape(16, 256, 256),
    )
    return hand_over(result).reshape(front_tiles.shape)


def solution(mesh):
    in_specs = (
        P(None, "row", None, None, "col", None),
        P("row", "col", None, None, None),
        P("row", "col", None, None),
        P(),
    )
    out_specs = P(None, "row", None, None, "col", None)
    return jax.shard_map(shards, mesh=mesh, in_specs=in_specs, out_specs=out_specs, check_vma=False)
```

```python
import jax
import jax.numpy as jnp
from jax import lax
from jax.experimental import pallas as pl
from jax.experimental.pallas import tpu as pltpu
from jax.sharding import PartitionSpec as P

MESH = pl.DeviceIdType.MESH
DMA = pltpu.SemaphoreType.DMA
ANY = pl.BlockSpec(memory_space=pl.ANY)
VMEM = pl.BlockSpec(memory_space=pltpu.VMEM)
SMEM = pl.BlockSpec(memory_space=pltpu.SMEM)
F32 = jnp.float32
BF16 = jnp.bfloat16

SQUARE = tuple((a, (a + s) % 4) for s in (1, 3, 0, 2) for a in (1, 3, 0, 2) if (a, s) != (0, 0))
PLANE = (
    (0, 1), (1, 0), (0, 3), (3, 0), (1, 1), (3, 3), (1, 3), (3, 1),
    (0, 2), (2, 0), (1, 2), (2, 1), (3, 2), (2, 3), (2, 2),
)
COLUMN = ((0, 1), (1, 0), (3, 0), (1, 1), (3, 1), (2, 0), (2, 1))
STEP = (1, 3, 2)
SHIFT = (0, -1, 1, 2)
WINDOW = 6
LOOSE_STEPS = 3


class Place:
    def __init__(self):
        self.r = lax.axis_index("row")
        self.c = lax.axis_index("col")
        self.z, self.x = self.r // 4, self.r % 4
        self.y, self.k = self.c // 2, self.c % 2

    def row(self, dz, dx):
        return (self.z + dz + 4) % 4 * 4 + (self.x + dx + 4) % 4

    def col(self, dy, dk):
        return (self.y + dy + 4) % 4 * 2 + (self.k + dk + 2) % 2


def remote(src, dst, send, recv, device):
    return pltpu.make_async_remote_copy(
        src_ref=src, dst_ref=dst, send_sem=send, recv_sem=recv, device_id=device, device_id_type=MESH
    )


def greet(me):
    barrier = pltpu.get_barrier_semaphore()
    for dz, dx in PLANE:
        pl.semaphore_signal(barrier, inc=1, device_id=(me.row(dz, dx), me.c), device_id_type=MESH)
    for dy, dk in COLUMN:
        pl.semaphore_signal(barrier, inc=1, device_id=(me.r, me.col(dy, dk)), device_id_type=MESH)
    pl.semaphore_wait(barrier, len(PLANE) + len(COLUMN))


class Children:
    def __init__(self, me, tiles, spots, mid, mid_spots, landed, landed_spots, sems):
        self.me, self.tiles, self.spots = me, tiles, spots
        self.mid, self.mid_spots, self.landed, self.landed_spots = mid, mid_spots, landed, landed_spots
        (
            self.own, self.own_spot, self.send1, self.recv1, self.spot_send1, self.spot_recv1,
            self.send2, self.recv2, self.spot_send2, self.spot_recv2,
        ) = sems

    def first(self, index):
        target = self.me.row(*SQUARE[index])
        device = (target, self.me.c)
        r = self.me.r
        return (
            remote(self.tiles.at[target], self.mid.at[r], self.send1.at[index], self.recv1.at[index], device),
            remote(
                self.spots, self.mid_spots.at[r], self.spot_send1.at[index], self.spot_recv1.at[index], device
            ),
        )

    def source(self, index):
        if index == len(SQUARE):
            return self.me.r, self.tiles.at[self.me.r], self.spots
        dz, dx = SQUARE[index]
        source = self.me.row(-dz, -dx)
        return source, self.mid.at[source], self.mid_spots.at[source]

    def _second(self, index, away):
        source, tile, spot = self.source(index)
        half = source // 8
        place = half * 8 + self.me.c
        if not away:
            return (
                pltpu.make_async_copy(tile, self.landed.at[place], self.own.at[half]),
                pltpu.make_async_copy(spot, self.landed_spots.at[place], self.own_spot.at[half]),
            )
        device = (self.me.r, source % 8)
        return (
            remote(tile, self.landed.at[place], self.send2.at[index], self.recv2.at[place], device),
            remote(
                spot, self.landed_spots.at[place], self.spot_send2.at[index], self.spot_recv2.at[place], device
            ),
        )

    def pass_on(self, index):
        if index < len(SQUARE):
            for copy in self.first(index):
                copy.wait_recv()
        col = self.source(index)[0] % 8

        @pl.when(col == self.me.c)
        def _():
            for copy in self._second(index, False):
                copy.start()

        @pl.when(col != self.me.c)
        def _():
            for copy in self._second(index, True):
                copy.start()

    def send(self):
        last = len(SQUARE)
        for index in range(last):
            if index == WINDOW:
                self.pass_on(last)
            if index >= WINDOW:
                self.pass_on(index - WINDOW)
            for copy in self.first(index):
                copy.start()
        for index in range(last - WINDOW, last):
            self.pass_on(index)

    def first_half(self):
        def rank(value):
            return jnp.where(value == 1, 0, jnp.where(value == 3, 1, jnp.where(value == 0, 2, 3)))

        steps = []
        for half in range(2):
            source = self.me.c + 8 * half
            dz, dx = (self.me.z - source // 4 + 4) % 4, (self.me.x - source % 4 + 4) % 4
            step = 4 * rank((dx - dz + 4) % 4) + rank(dz)
            steps.append(jnp.where(source == self.me.r, -1, step))
        return jnp.where(steps[0] < steps[1], 0, 1)

    def arrive(self, half, dy, dk):
        place = half * 8 + self.me.col(dy, dk)
        tile, spot = self.landed.at[place], self.landed_spots.at[place]
        if (dy, dk) == (0, 0):
            pltpu.make_async_copy(tile, tile, self.own.at[half]).wait()
            pltpu.make_async_copy(spot, spot, self.own_spot.at[half]).wait()
        else:
            device = (self.me.r, self.me.c)
            remote(tile, tile, self.send2.at[0], self.recv2.at[place], device).wait_recv()
            remote(spot, spot, self.spot_send2.at[0], self.spot_recv2.at[place], device).wait_recv()
        return place

    def drain(self):
        for index in range(len(SQUARE) + 1):
            if index < len(SQUARE):
                for copy in self.first(index):
                    copy.wait_send()
            col = self.source(index)[0] % 8

            @pl.when(col != self.me.c)
            def _(index=index):
                for copy in self._second(index, True):
                    copy.wait_send()


class PlaneGather:
    def __init__(self, me, at, own, x_first, relayed, sems):
        self.me, self.at, self.own, self.x_first = me, at, own, x_first
        self.send1, self.recv1, self.send2, self.recv2 = sems
        self.relayed = relayed
        self.near = range(2 if relayed else 3)
        self.far = (2, 3) if relayed else (2,)

    def number(self, one, two):
        return self.me.row(two, one) if self.x_first else self.me.row(one, two)

    def _copy(self, index, own, source, landed, send, recv, targets):
        block, landed = self.at(source) if own is None else own, self.at(landed)
        if self.relayed and index >= 2:
            half = pl.ds(2 * (index - 2), 2)
            block, landed = self.at(source).at[half], landed.at[half]
            index -= 2
        return remote(block, landed, send, recv, (targets[index], self.me.c))

    def _first(self, index, source, landed):
        targets = [self.number(step, 0) for step in (1, -1, 2)]
        return self._copy(
            index, self.own, source, landed, self.send1.at[index], self.recv1.at[index], targets
        )

    def _second(self, which, index, source, landed):
        targets = [self.number(0, step) for step in (1, -1, 2)]
        slot = which * 4 + index
        return self._copy(
            index, None if which else self.own, source, landed,
            self.send2.at[slot], self.recv2.at[slot], targets,
        )

    def start(self):
        for index in self.near:
            self._first(index, self.me.r, self.me.r).start()

    def relay(self):
        for index, shift in enumerate((-1, 1)):
            source = self.number(shift, 0)
            self._first(index, self.me.r, source).wait_recv()
            if self.relayed:
                self._first(index + 2, source, source).start()

    def forward(self, which):
        source = self.number(SHIFT[which], 0)
        if which == 3:
            for index in self.far:
                self._first(index, source, source).wait_recv()
        for index in self.near:
            self._second(which, index, source, source).start()
        return source

    def relay_second(self, which):
        landed = []
        for index, shift in enumerate((-1, 1)):
            source = self.number(SHIFT[which], shift)
            self._second(which, index, source, source).wait_recv()
            if self.relayed:
                self._second(which, index + 2, source, source).start()
            landed.append(source)
        return landed

    def finish(self, which):
        source = self.number(SHIFT[which], 2)
        for index in self.far:
            self._second(which, index, source, source).wait_recv()
        return source

    def drain(self):
        messages = (*range(2), *self.far)
        for index in messages:
            self._first(index, self.me.r, self.me.r).wait_send()
        for which in range(4):
            for index in messages:
                self._second(which, index, self.me.r, self.me.r).wait_send()


def split(value):
    high = value.astype(BF16)
    return high, (value - high.astype(F32)).astype(BF16)


def dot1(a, b):
    return jnp.dot(a, b, preferred_element_type=F32)


def dot3(a, b):
    return dot1(a[0], b[0]) + (dot1(a[0], b[1]) + dot1(a[1], b[0]))


def invert(block, block_high, block_low, estimate):
    size = block.shape[0]
    diagonal = lax.broadcasted_iota(jnp.int32, (size, size), 0) == lax.broadcasted_iota(
        jnp.int32, (size, size), 1
    )
    value = block[...]
    block_high[...], block_low[...] = split(value)
    weights = jnp.where(diagonal, value, 0.0)
    by_row = 1.0 / jnp.sum(weights, axis=1, keepdims=True)
    by_col = 1.0 / jnp.sum(weights, axis=0, keepdims=True)
    estimate[...] = jnp.where(diagonal, by_col, -(by_row * value * by_col))

    def loose(step, carry):
        now = estimate[...]
        high = now.astype(BF16)
        product = dot1(block_high[...], high)
        estimate[...] = 2.0 * now - dot1(high, product.astype(BF16))
        return carry

    def residual(halves):
        return jnp.where(diagonal, 1.0, 0.0) - dot3((block_high[...], block_low[...]), halves)

    lax.fori_loop(0, LOOSE_STEPS, loose, 0)
    now = estimate[...]
    halves = split(now)
    estimate[...] = now + dot1(halves[0], residual(halves).astype(BF16))
    now = estimate[...]
    halves = split(now)
    estimate[...] = now + dot3(halves, split(residual(halves)))


def pivot_kernel(
    panel, targets, front_in, tiles, out, mid_spots, mid, spots, landed, landed_spots, m, front, result, rows, cols, ug, bg, cg, upc, cpc, bsc, bpc,
    block, block_high, block_low, x1, x2, l1, l2, c2, lt_high, lt_low, own,
    row_s, row_r, col_s, col_r, bs_s, bs_r, bc_s, bc_r, c_s, c_r, cx_s, cx_r, ua, ub, ba, bb, bx_s, bx_r,
    out_sem, child_sems,
):
    me = Place()
    greet(me)
    pivots = [panel[j // 2, j % 2] for j in range(4)]

    spots[...] = jnp.zeros_like(spots)
    spots[0:1, 0:16] = targets[0:1, :] // 16 * 4 + targets[1:2, :] // 8
    children = Children(me, tiles, spots, mid, mid_spots, landed, landed_spots, child_sems)
    brought = [
        pltpu.make_async_copy(front_in.at[pl.ds(512 * i, 512)], front.at[pl.ds(512 * i, 512)], out_sem.at[i])
        for i in range(8)
    ]
    children.send()
    for copy in brought:
        copy.start()
    for copy in brought:
        copy.wait()
    for chunk in range(8):
        part = front[pl.ds(chunk, 512, stride=8), :].reshape(2, 256, 128)
        m[:, chunk // 2, :, pl.ds(chunk % 2 * 128, 128)] = part
    lane = lax.broadcasted_iota(jnp.int32, (8, 128), 1)
    first_half = children.first_half()
    for half in (first_half, 1 - first_half):
        for group in (((0, 0), *COLUMN[:3]), COLUMN[3:]):
            places = [children.arrive(half, dy, dk) for dy, dk in group]
            spot = []
            for place in places:
                mine = jnp.where(lane == me.r, landed_spots[place], 0)
                spot.append(jnp.sum(mine.astype(F32), keepdims=True).astype(jnp.int32))

            def add(slot, carry, places=places, spot=spot):
                parts = [jnp.where(s == slot, landed[p], 0.0) for s, p in zip(spot, places)]
                m[slot // 4, slot % 4] += (parts[0] + parts[1]) + (parts[2] + parts[3])
                return carry

            lax.fori_loop(0, 8, add, 0)

    def row_slice(target):
        return m.at[:, :, pl.ds(pl.multiple_of(target * 16, 16), 16), :]

    def col_slice(target):
        return m.at[target // 4, :, pl.ds(pl.multiple_of(target % 4 * 64, 64), 64), :]

    def row_spread(index):
        target = me.row(*PLANE[index])
        return lambda source: remote(
            row_slice(target), rows.at[source], row_s.at[index], row_r.at[index], (target, me.c)
        )

    def col_spread(index):
        target = me.col(*COLUMN[index])
        return lambda source: remote(
            col_slice(target), cols.at[source], col_s.at[index], col_r.at[index], (me.r, target)
        )

    for index in range(15):
        row_spread(index)(me.r).start()
        if index < 7:
            col_spread(index)(me.c).start()
    mine = (
        pltpu.make_async_copy(row_slice(me.r), rows.at[me.r], own.at[0]),
        pltpu.make_async_copy(col_slice(me.c), cols.at[me.c], own.at[1]),
    )
    for copy in mine:
        copy.start()
    for copy in mine:
        copy.wait()
    for index, (dz, dx) in enumerate(PLANE):
        row_spread(index)(me.row(-dz, -dx)).wait_recv()
    for j, pivot in enumerate(pivots):
        upc[:, j] = rows[pivot % 16, pivot // 16]

    def b_rows(col):
        return upc.at[:, col // 2, pl.ds(pl.multiple_of(col % 2 * 8, 8), 8), :]

    def b_scatter(index):
        target = me.col(*COLUMN[index])
        return lambda source: remote(
            b_rows(target), bsc.at[source], bs_s.at[index], bs_r.at[index], (me.r, target)
        )

    for index in range(7):
        b_scatter(index)(me.c).start()
    own_scatter = pltpu.make_async_copy(b_rows(me.c), bsc.at[me.c], own.at[2])
    own_scatter.start()

    def u_at(first):
        return lambda source: ug.at[:, pl.ds(first, 2), source]

    u1 = PlaneGather(me, u_at(0), upc.at[:, pl.ds(0, 2)], True, True, ua)
    u2 = PlaneGather(me, u_at(2), upc.at[:, pl.ds(2, 2)], False, True, ub)
    u1.start()
    u2.start()
    own_u = pltpu.make_async_copy(upc, ug.at[:, :, me.r], own.at[3])
    own_u.start()

    own_scatter.wait()
    for index, (dy, dk) in enumerate(COLUMN):
        b_scatter(index)(me.col(-dy, -dk)).wait_recv()
    for j, pivot in enumerate(pivots):
        bpc[j] = bsc[pivot % 8, pivot // 8]

    def b_piece(col):
        return bg.at[:, col // 2, me.r, pl.ds(pl.multiple_of(col % 2 * 8, 8), 8), :]

    def b_gather(index):
        return lambda source: remote(
            bpc, b_piece(source), bc_s.at[index], bc_r.at[index], (me.r, me.col(*COLUMN[index]))
        )

    for index in range(7):
        b_gather(index)(me.c).start()
    own_b = pltpu.make_async_copy(bpc, b_piece(me.c), own.at[4])
    own_b.start()

    for index, (dy, dk) in enumerate(COLUMN):
        col_spread(index)(me.col(-dy, -dk)).wait_recv()
    for j, pivot in enumerate(pivots):
        cpc[j] = cols[pivot % 8, pivot // 8]

    def c_out(index):
        return lambda source: remote(
            cpc, cg.at[source], c_s.at[index], c_r.at[index], (me.r, me.col(STEP[index], 0))
        )

    def c_swap(which):
        source = me.col(-STEP[which - 1] if which else 0, 0)
        src = cg.at[source] if which else cpc
        return lambda landed: remote(
            src, cg.at[landed], cx_s.at[which], cx_r.at[which], (me.r, me.col(0, 1))
        )

    own_b.wait()
    for index, (dy, dk) in enumerate(COLUMN):
        b_gather(index)(me.col(-dy, -dk)).wait_recv()

    def b_at(pivot):
        return lambda source: bg.at[:, pivot, source]

    b1 = PlaneGather(me, b_at(me.k), b_at(me.k)(me.r), True, False, ba)
    b2 = PlaneGather(me, b_at(2 + me.k), b_at(2 + me.k)(me.r), False, False, bb)
    b1.start()
    b2.start()

    def b_swap(half, slot, source, back):
        pivot = 2 * half + (1 - me.k if back else me.k)
        block = bg.at[:, pivot, source]
        return remote(block, block, bx_s.at[half, slot], bx_r.at[half, slot], (me.r, me.col(0, 1)))

    for gather in (b1, b2):
        gather.forward(0)
    for index in range(3):
        c_out(index)(me.c).start()
    c_swap(0)(me.c).start()
    own_c = pltpu.make_async_copy(cpc, cg.at[me.c], own.at[5])
    own_c.start()

    for gather in (u1, u2, b1, b2):
        gather.relay()
    for which in range(1, 4):
        for half, gather in enumerate((b1, b2)):
            source = gather.forward(which)
            b_swap(half, which - 1, source, False).start()
    for which in range(4):
        for gather in (u1, u2):
            gather.forward(which)
    for which in range(4):
        for half, gather in enumerate((b1, b2)):
            for index, source in enumerate(gather.relay_second(which)):
                b_swap(half, 3 + which * 3 + index, source, False).start()
    for which in range(1, 4):
        source = me.col(-STEP[which - 1], 0)
        c_out(which - 1)(source).wait_recv()
        c_swap(which)(source).start()
    for gather in (u1, u2):
        gather.relay_second(0)
    for half, gather in enumerate((b1, b2)):
        for which in range(4):
            source = gather.finish(which)
            b_swap(half, 5 + which * 3, source, False).start()

    def b_arrived(half, gather):
        for which in range(4):
            if which:
                source = gather.number(SHIFT[which], 0)
                b_swap(half, which - 1, source, True).wait_recv()
            for index, shift in enumerate((-1, 1, 2)):
                source = gather.number(SHIFT[which], shift)
                b_swap(half, 3 + which * 3 + index, source, True).wait_recv()

    def u_relay(which):
        for gather in (u1, u2):
            gather.relay_second(which)

    row_tile = (lax.broadcasted_iota(jnp.int32, (512, 1), 0) // 256) * 16 + me.r
    in1 = (row_tile == pivots[0]) | (row_tile == pivots[1])
    in2 = (row_tile == pivots[2]) | (row_tile == pivots[3])

    def b_part(rows, cols):
        return jnp.concatenate(
            [bg[2 * cols + j, pl.ds(2 * rows, 2)].reshape(512, 256) for j in range(2)], axis=1
        )

    def c_part(cols):
        return jnp.concatenate([cg[:, 2 * cols + j].reshape(512, 256) for j in range(2)], axis=1)

    b_arrived(0, b1)
    block[...] = b_part(0, 0)
    u_relay(1)
    invert(block, block_high, block_low, x1)
    b_arrived(1, b2)
    u_relay(2)
    x1_halves = split(x1[...])
    b12 = split(b_part(0, 1))
    t_halves = split(dot3(split(b_part(1, 0)), x1_halves))
    block[...] = b_part(1, 1) - dot3(t_halves, b12)
    u_relay(3)
    own_c.wait()
    for which in range(4):
        c_swap(which)(me.col(-STEP[which - 1] if which else 0, 1)).wait_recv()
    lower = dot3(split(c_part(0)), x1_halves)
    l1[...] = lower
    lower = jnp.where(in1, 0.0, lower)
    c2[...] = c_part(1) - dot3(split(lower), b12)
    invert(block, block_high, block_low, x2)
    lower2 = dot3(split(c2[...]), split(x2[...]))
    l2[...] = lower2
    lower2 = jnp.where(in1 | in2, 0.0, lower2)
    halves = split(lower2)
    lt_high[:, 512:], lt_low[:, 512:] = halves
    lt_high[:, :512], lt_low[:, :512] = split(lower - dot3(halves, t_halves))

    own_u.wait()
    for which in range(4):
        for gather in (u1, u2):
            gather.finish(which)
    for b in range(4):
        update = dot3((lt_high[...], lt_low[...]), split(ug[b].reshape(1024, 256)))
        col_tile = b * 8 + me.c
        new = m[:, b].reshape(512, 256) - update
        for j in range(4):
            window = slice(j % 2 * 256, j % 2 * 256 + 256)
            if j < 2:
                column = jnp.where(in1, cg[:, j].reshape(512, 256), l1[:, window])
            else:
                column = jnp.where(in1 | in2, c2[:, window], l2[:, window])
            new = jnp.where(col_tile == pivots[j], column, new)
        for half in range(2):
            result[pl.ds(2 * b + half, 512, stride=8), :] = new[:, half * 128 : half * 128 + 128]

    written = [
        pltpu.make_async_copy(result.at[pl.ds(512 * i, 512)], out.at[pl.ds(512 * i, 512)], out_sem.at[i])
        for i in range(8)
    ]
    for copy in written:
        copy.start()
    children.drain()
    for index in range(15):
        row_spread(index)(me.r).wait_send()
    for index in range(7):
        col_spread(index)(me.c).wait_send()
        b_scatter(index)(me.c).wait_send()
        b_gather(index)(me.c).wait_send()
    for index in range(3):
        c_out(index)(me.c).wait_send()
    for which in range(4):
        c_swap(which)(me.c).wait_send()
    for gather in (u1, u2, b1, b2):
        gather.drain()
    for half in range(2):
        for slot in range(15):
            b_swap(half, slot, me.r, False).wait_send()
    for copy in written:
        copy.wait()


def eliminate(panel, targets, front, tiles):
    plane = [DMA((4,)), DMA((4,)), DMA((16,)), DMA((16,))]
    square = pltpu.VMEM((512, 512), F32)
    narrow = pltpu.VMEM((512, 512), BF16)
    return pl.pallas_call(
        pivot_kernel,
        name="pivots",
        out_shape=[
            jax.ShapeDtypeStruct((4096, 128), F32),
            jax.ShapeDtypeStruct((16, 8, 128), jnp.int32),
        ],
        in_specs=[SMEM, VMEM, ANY, ANY],
        out_specs=[ANY] * 2,
        scratch_shapes=[
            pltpu.VMEM((16, 256, 256), F32),
            pltpu.VMEM((8, 128), jnp.int32),
            pltpu.VMEM((16, 256, 256), F32),
            pltpu.VMEM((16, 8, 128), jnp.int32),
            pltpu.VMEM((2, 4, 256, 256), F32),
            pltpu.VMEM((4096, 128), F32),
            pltpu.VMEM((4096, 128), F32),
            pltpu.VMEM((16, 2, 4, 16, 256), F32),
            pltpu.VMEM((8, 4, 64, 256), F32),
            pltpu.VMEM((4, 4, 16, 16, 256), F32),
            pltpu.VMEM((4, 4, 16, 16, 256), F32),
            pltpu.VMEM((8, 4, 64, 256), F32),
            pltpu.VMEM((4, 4, 16, 256), F32),
            pltpu.VMEM((4, 64, 256), F32),
            pltpu.VMEM((8, 4, 8, 256), F32),
            pltpu.VMEM((4, 8, 256), F32),
            square, narrow, narrow, square, square, square, square, square,
            pltpu.VMEM((512, 1024), BF16), pltpu.VMEM((512, 1024), BF16),
            DMA((7,)),
            DMA((15,)), DMA((15,)), DMA((7,)), DMA((7,)),
            DMA((7,)), DMA((7,)), DMA((7,)), DMA((7,)),
            DMA((3,)), DMA((3,)), DMA((4,)), DMA((4,)),
            plane, plane, plane, plane,
            DMA((2, 15)), DMA((2, 15)),
            DMA((8,)), [DMA((2,)), DMA((2,))] + [DMA((16,))] * 8,
        ],
        compiler_params=pltpu.CompilerParams(
            collective_id=0, has_side_effects=True, vmem_limit_bytes=56 * 2**20
        ),
    )(panel, targets, front, tiles)[0]


def hand_over_kernel(source, out, held, sems):
    def copies(step):
        refs = ((source, held), (held, out))[step]
        for i in range(8):
            part = pl.ds(4096 // 8 * i, 4096 // 8)
            yield pltpu.make_async_copy(refs[0].at[part], refs[1].at[part], sems.at[step, i])

    for copy in copies(0):
        copy.start()
    for brought, written in zip(copies(0), copies(1)):
        brought.wait()
        written.start()
    for copy in copies(1):
        copy.wait()


def hand_over(result):
    return pl.pallas_call(
        hand_over_kernel,
        name="hand_over",
        out_shape=jax.ShapeDtypeStruct(result.shape, result.dtype),
        in_specs=[ANY],
        out_specs=ANY,
        scratch_shapes=[pltpu.VMEM(result.shape, result.dtype), DMA((2, 8))],
        compiler_params=pltpu.CompilerParams(vmem_limit_bytes=60 * 2**20),
    )(result)


def shards(front_tiles, child_tiles, child_target, panel_tiles):
    result = eliminate(
        panel_tiles,
        child_target.reshape(16, 2).T,
        front_tiles.reshape(4096, 128),
        child_tiles.reshape(16, 256, 256),
    )
    return hand_over(result).reshape(front_tiles.shape)


def solution(mesh):
    in_specs = (
        P(None, "row", None, None, "col", None),
        P("row", "col", None, None, None),
        P("row", "col", None, None),
        P(),
    )
    out_specs = P(None, "row", None, None, "col", None)
    return jax.shard_map(shards, mesh=mesh, in_specs=in_specs, out_specs=out_specs, check_vma=False)
```

```python
import jax
import jax.numpy as jnp
from jax import lax
from jax.experimental import pallas as pl
from jax.experimental.pallas import tpu as pltpu
from jax.sharding import PartitionSpec as P

MESH = pl.DeviceIdType.MESH
DMA = pltpu.SemaphoreType.DMA
ANY = pl.BlockSpec(memory_space=pl.ANY)
VMEM = pl.BlockSpec(memory_space=pltpu.VMEM)
SMEM = pl.BlockSpec(memory_space=pltpu.SMEM)
F32 = jnp.float32
BF16 = jnp.bfloat16

SQUARE = tuple((a, (a + s) % 4) for s in (1, 3, 0, 2) for a in (1, 3, 0, 2) if (a, s) != (0, 0))
PLANE = (
    (0, 1), (1, 0), (0, 3), (3, 0), (1, 1), (3, 3), (1, 3), (3, 1),
    (0, 2), (2, 0), (1, 2), (2, 1), (3, 2), (2, 3), (2, 2),
)
COLUMN = ((0, 1), (1, 0), (3, 0), (1, 1), (3, 1), (2, 0), (2, 1))
STEP = (1, 3, 2)
SHIFT = (0, -1, 1, 2)
WINDOW = 6
LOOSE_STEPS = 3


class Place:
    def __init__(self):
        self.r = lax.axis_index("row")
        self.c = lax.axis_index("col")
        self.z, self.x = self.r // 4, self.r % 4
        self.y, self.k = self.c // 2, self.c % 2

    def row(self, dz, dx):
        return (self.z + dz + 4) % 4 * 4 + (self.x + dx + 4) % 4

    def col(self, dy, dk):
        return (self.y + dy + 4) % 4 * 2 + (self.k + dk + 2) % 2


def remote(src, dst, send, recv, device):
    return pltpu.make_async_remote_copy(
        src_ref=src, dst_ref=dst, send_sem=send, recv_sem=recv, device_id=device, device_id_type=MESH
    )


def greet(me):
    barrier = pltpu.get_barrier_semaphore()
    for dz, dx in PLANE:
        pl.semaphore_signal(barrier, inc=1, device_id=(me.row(dz, dx), me.c), device_id_type=MESH)
    for dy, dk in COLUMN:
        pl.semaphore_signal(barrier, inc=1, device_id=(me.r, me.col(dy, dk)), device_id_type=MESH)
    pl.semaphore_wait(barrier, len(PLANE) + len(COLUMN))


class Children:
    def __init__(self, me, tiles, spots, mid, mid_spots, landed, landed_spots, sems):
        self.me, self.tiles, self.spots = me, tiles, spots
        self.mid, self.mid_spots, self.landed, self.landed_spots = mid, mid_spots, landed, landed_spots
        (
            self.own, self.own_spot, self.send1, self.recv1, self.spot_send1, self.spot_recv1,
            self.send2, self.recv2, self.spot_send2, self.spot_recv2,
        ) = sems

    def first(self, index):
        target = self.me.row(*SQUARE[index])
        device = (target, self.me.c)
        r = self.me.r
        return (
            remote(self.tiles.at[target], self.mid.at[r], self.send1.at[index], self.recv1.at[index], device),
            remote(
                self.spots, self.mid_spots.at[r], self.spot_send1.at[index], self.spot_recv1.at[index], device
            ),
        )

    def source(self, index):
        if index == len(SQUARE):
            return self.me.r, self.tiles.at[self.me.r], self.spots
        dz, dx = SQUARE[index]
        source = self.me.row(-dz, -dx)
        return source, self.mid.at[source], self.mid_spots.at[source]

    def _second(self, index, away):
        source, tile, spot = self.source(index)
        half = source // 8
        place = half * 8 + self.me.c
        if not away:
            return (
                pltpu.make_async_copy(tile, self.landed.at[place], self.own.at[half]),
                pltpu.make_async_copy(spot, self.landed_spots.at[place], self.own_spot.at[half]),
            )
        device = (self.me.r, source % 8)
        return (
            remote(tile, self.landed.at[place], self.send2.at[index], self.recv2.at[place], device),
            remote(
                spot, self.landed_spots.at[place], self.spot_send2.at[index], self.spot_recv2.at[place], device
            ),
        )

    def pass_on(self, index):
        if index < len(SQUARE):
            for copy in self.first(index):
                copy.wait_recv()
        col = self.source(index)[0] % 8

        @pl.when(col == self.me.c)
        def _():
            for copy in self._second(index, False):
                copy.start()

        @pl.when(col != self.me.c)
        def _():
            for copy in self._second(index, True):
                copy.start()

    def send(self):
        last = len(SQUARE)
        for index in range(last):
            if index == WINDOW:
                self.pass_on(last)
            if index >= WINDOW:
                self.pass_on(index - WINDOW)
            for copy in self.first(index):
                copy.start()
        for index in range(last - WINDOW, last):
            self.pass_on(index)

    def first_half(self):
        def rank(value):
            return jnp.where(value == 1, 0, jnp.where(value == 3, 1, jnp.where(value == 0, 2, 3)))

        steps = []
        for half in range(2):
            source = self.me.c + 8 * half
            dz, dx = (self.me.z - source // 4 + 4) % 4, (self.me.x - source % 4 + 4) % 4
            step = 4 * rank((dx - dz + 4) % 4) + rank(dz)
            steps.append(jnp.where(source == self.me.r, -1, step))
        return jnp.where(steps[0] < steps[1], 0, 1)

    def arrive(self, half, dy, dk):
        place = half * 8 + self.me.col(dy, dk)
        tile, spot = self.landed.at[place], self.landed_spots.at[place]
        if (dy, dk) == (0, 0):
            pltpu.make_async_copy(tile, tile, self.own.at[half]).wait()
            pltpu.make_async_copy(spot, spot, self.own_spot.at[half]).wait()
        else:
            device = (self.me.r, self.me.c)
            remote(tile, tile, self.send2.at[0], self.recv2.at[place], device).wait_recv()
            remote(spot, spot, self.spot_send2.at[0], self.spot_recv2.at[place], device).wait_recv()
        return place

    def drain(self):
        for index in range(len(SQUARE) + 1):
            if index < len(SQUARE):
                for copy in self.first(index):
                    copy.wait_send()
            col = self.source(index)[0] % 8

            @pl.when(col != self.me.c)
            def _(index=index):
                for copy in self._second(index, True):
                    copy.wait_send()


class PlaneGather:
    def __init__(self, me, at, own, x_first, relayed, sems):
        self.me, self.at, self.own, self.x_first = me, at, own, x_first
        self.send1, self.recv1, self.send2, self.recv2 = sems
        self.relayed = relayed
        self.near = range(2 if relayed else 3)
        self.far = (2, 3) if relayed else (2,)

    def number(self, one, two):
        return self.me.row(two, one) if self.x_first else self.me.row(one, two)

    def _copy(self, index, own, source, landed, send, recv, targets):
        block, landed = self.at(source) if own is None else own, self.at(landed)
        if self.relayed and index >= 2:
            half = pl.ds(2 * (index - 2), 2)
            block, landed = self.at(source).at[half], landed.at[half]
            index -= 2
        return remote(block, landed, send, recv, (targets[index], self.me.c))

    def _first(self, index, source, landed):
        targets = [self.number(step, 0) for step in (1, -1, 2)]
        return self._copy(
            index, self.own, source, landed, self.send1.at[index], self.recv1.at[index], targets
        )

    def _second(self, which, index, source, landed):
        targets = [self.number(0, step) for step in (1, -1, 2)]
        slot = which * 4 + index
        return self._copy(
            index, None if which else self.own, source, landed,
            self.send2.at[slot], self.recv2.at[slot], targets,
        )

    def start(self):
        for index in self.near:
            self._first(index, self.me.r, self.me.r).start()

    def relay(self):
        for index, shift in enumerate((-1, 1)):
            source = self.number(shift, 0)
            self._first(index, self.me.r, source).wait_recv()
            if self.relayed:
                self._first(index + 2, source, source).start()

    def forward(self, which):
        source = self.number(SHIFT[which], 0)
        if which == 3:
            for index in self.far:
                self._first(index, source, source).wait_recv()
        for index in self.near:
            self._second(which, index, source, source).start()
        return source

    def relay_second(self, which):
        landed = []
        for index, shift in enumerate((-1, 1)):
            source = self.number(SHIFT[which], shift)
            self._second(which, index, source, source).wait_recv()
            if self.relayed:
                self._second(which, index + 2, source, source).start()
            landed.append(source)
        return landed

    def finish(self, which):
        source = self.number(SHIFT[which], 2)
        for index in self.far:
            self._second(which, index, source, source).wait_recv()
        return source

    def drain(self):
        messages = (*range(2), *self.far)
        for index in messages:
            self._first(index, self.me.r, self.me.r).wait_send()
        for which in range(4):
            for index in messages:
                self._second(which, index, self.me.r, self.me.r).wait_send()


def split(value):
    high = value.astype(BF16)
    return high, (value - high.astype(F32)).astype(BF16)


def dot1(a, b):
    return jnp.dot(a, b, preferred_element_type=F32)


def dot3(a, b):
    return dot1(a[0], b[0]) + (dot1(a[0], b[1]) + dot1(a[1], b[0]))


def invert(block, block_high, block_low, estimate):
    size = block.shape[0]
    diagonal = lax.broadcasted_iota(jnp.int32, (size, size), 0) == lax.broadcasted_iota(
        jnp.int32, (size, size), 1
    )
    value = block[...]
    block_high[...], block_low[...] = split(value)
    weights = jnp.where(diagonal, value, 0.0)
    by_row = 1.0 / jnp.sum(weights, axis=1, keepdims=True)
    by_col = 1.0 / jnp.sum(weights, axis=0, keepdims=True)
    estimate[...] = jnp.where(diagonal, by_col, -(by_row * value * by_col))

    def loose(step, carry):
        now = estimate[...]
        high = now.astype(BF16)
        product = dot1(block_high[...], high)
        estimate[...] = 2.0 * now - dot1(high, product.astype(BF16))
        return carry

    def residual(halves):
        return jnp.where(diagonal, 1.0, 0.0) - dot3((block_high[...], block_low[...]), halves)

    lax.fori_loop(0, LOOSE_STEPS, loose, 0)
    now = estimate[...]
    halves = split(now)
    estimate[...] = now + dot1(halves[0], residual(halves).astype(BF16))
    now = estimate[...]
    halves = split(now)
    estimate[...] = now + dot3(halves, split(residual(halves)))


def pivot_kernel(
    panel, targets, front_in, tiles, out, mid_spots, mid, spots, landed, landed_spots, m, front, result, rows, cols, ug, bg, cg, upc, cpc, bsc, bpc,
    block, block_high, block_low, x1, x2, l1, l2, c2, lt_high, lt_low, own,
    row_s, row_r, col_s, col_r, bs_s, bs_r, bc_s, bc_r, c_s, c_r, cx_s, cx_r, ua, ub, ba, bb, bx_s, bx_r,
    out_sem, child_sems,
):
    me = Place()
    greet(me)
    pivots = [panel[j // 2, j % 2] for j in range(4)]

    spots[...] = jnp.zeros_like(spots)
    spots[0:1, 0:16] = targets[0:1, :] // 16 * 4 + targets[1:2, :] // 8
    children = Children(me, tiles, spots, mid, mid_spots, landed, landed_spots, child_sems)
    brought = [
        pltpu.make_async_copy(front_in.at[pl.ds(512 * i, 512)], front.at[pl.ds(512 * i, 512)], out_sem.at[i])
        for i in range(8)
    ]
    children.send()
    for copy in brought:
        copy.start()
    for copy in brought:
        copy.wait()
    for chunk in range(8):
        part = front[pl.ds(chunk, 512, stride=8), :].reshape(2, 256, 128)
        m[:, chunk // 2, :, pl.ds(chunk % 2 * 128, 128)] = part
    lane = lax.broadcasted_iota(jnp.int32, (8, 128), 1)
    first_half = children.first_half()
    for half in (first_half, 1 - first_half):
        for group in (((0, 0), *COLUMN[:3]), COLUMN[3:]):
            places = [children.arrive(half, dy, dk) for dy, dk in group]
            spot = []
            for place in places:
                mine = jnp.where(lane == me.r, landed_spots[place], 0)
                spot.append(jnp.sum(mine.astype(F32), keepdims=True).astype(jnp.int32))

            def add(slot, carry, places=places, spot=spot):
                parts = [jnp.where(s == slot, landed[p], 0.0) for s, p in zip(spot, places)]
                m[slot // 4, slot % 4] += (parts[0] + parts[1]) + (parts[2] + parts[3])
                return carry

            lax.fori_loop(0, 8, add, 0)

    def row_slice(target):
        return m.at[:, :, pl.ds(pl.multiple_of(target * 16, 16), 16), :]

    def col_slice(target):
        return m.at[target // 4, :, pl.ds(pl.multiple_of(target % 4 * 64, 64), 64), :]

    def row_spread(index):
        target = me.row(*PLANE[index])
        return lambda source: remote(
            row_slice(target), rows.at[source], row_s.at[index], row_r.at[index], (target, me.c)
        )

    def col_spread(index):
        target = me.col(*COLUMN[index])
        return lambda source: remote(
            col_slice(target), cols.at[source], col_s.at[index], col_r.at[index], (me.r, target)
        )

    for index in range(15):
        row_spread(index)(me.r).start()
        if index < 7:
            col_spread(index)(me.c).start()
    mine = (
        pltpu.make_async_copy(row_slice(me.r), rows.at[me.r], own.at[0]),
        pltpu.make_async_copy(col_slice(me.c), cols.at[me.c], own.at[1]),
    )
    for copy in mine:
        copy.start()
    for copy in mine:
        copy.wait()
    for index, (dz, dx) in enumerate(PLANE):
        row_spread(index)(me.row(-dz, -dx)).wait_recv()
    for j, pivot in enumerate(pivots):
        upc[:, j] = rows[pivot % 16, pivot // 16]

    def b_rows(col):
        return upc.at[:, col // 2, pl.ds(pl.multiple_of(col % 2 * 8, 8), 8), :]

    def b_scatter(index):
        target = me.col(*COLUMN[index])
        return lambda source: remote(
            b_rows(target), bsc.at[source], bs_s.at[index], bs_r.at[index], (me.r, target)
        )

    for index in range(7):
        b_scatter(index)(me.c).start()
    own_scatter = pltpu.make_async_copy(b_rows(me.c), bsc.at[me.c], own.at[2])
    own_scatter.start()

    def u_at(first):
        return lambda source: ug.at[:, pl.ds(first, 2), source]

    u1 = PlaneGather(me, u_at(0), upc.at[:, pl.ds(0, 2)], True, True, ua)
    u2 = PlaneGather(me, u_at(2), upc.at[:, pl.ds(2, 2)], False, True, ub)
    u1.start()
    u2.start()
    own_u = pltpu.make_async_copy(upc, ug.at[:, :, me.r], own.at[3])
    own_u.start()

    own_scatter.wait()
    for index, (dy, dk) in enumerate(COLUMN):
        b_scatter(index)(me.col(-dy, -dk)).wait_recv()
    for j, pivot in enumerate(pivots):
        bpc[j] = bsc[pivot % 8, pivot // 8]

    def b_piece(col):
        return bg.at[:, col // 2, me.r, pl.ds(pl.multiple_of(col % 2 * 8, 8), 8), :]

    def b_gather(index):
        return lambda source: remote(
            bpc, b_piece(source), bc_s.at[index], bc_r.at[index], (me.r, me.col(*COLUMN[index]))
        )

    for index in range(7):
        b_gather(index)(me.c).start()
    own_b = pltpu.make_async_copy(bpc, b_piece(me.c), own.at[4])
    own_b.start()

    for index, (dy, dk) in enumerate(COLUMN):
        col_spread(index)(me.col(-dy, -dk)).wait_recv()
    for j, pivot in enumerate(pivots):
        cpc[j] = cols[pivot % 8, pivot // 8]

    def c_out(index):
        return lambda source: remote(
            cpc, cg.at[source], c_s.at[index], c_r.at[index], (me.r, me.col(STEP[index], 0))
        )

    def c_swap(which):
        source = me.col(-STEP[which - 1] if which else 0, 0)
        src = cg.at[source] if which else cpc
        return lambda landed: remote(
            src, cg.at[landed], cx_s.at[which], cx_r.at[which], (me.r, me.col(0, 1))
        )

    own_b.wait()
    for index, (dy, dk) in enumerate(COLUMN):
        b_gather(index)(me.col(-dy, -dk)).wait_recv()

    def b_at(pivot):
        return lambda source: bg.at[:, pivot, source]

    b1 = PlaneGather(me, b_at(me.k), b_at(me.k)(me.r), True, True, ba)
    b2 = PlaneGather(me, b_at(2 + me.k), b_at(2 + me.k)(me.r), False, True, bb)
    b1.start()
    b2.start()

    def b_swap(half, slot, source, back):
        pivot = 2 * half + (1 - me.k if back else me.k)
        block = bg.at[:, pivot, source]
        return remote(block, block, bx_s.at[half, slot], bx_r.at[half, slot], (me.r, me.col(0, 1)))

    for gather in (b1, b2):
        gather.forward(0)
    for index in range(3):
        c_out(index)(me.c).start()
    c_swap(0)(me.c).start()
    own_c = pltpu.make_async_copy(cpc, cg.at[me.c], own.at[5])
    own_c.start()

    for gather in (u1, u2, b1, b2):
        gather.relay()
    for which in range(1, 4):
        for half, gather in enumerate((b1, b2)):
            source = gather.forward(which)
            b_swap(half, which - 1, source, False).start()
    for which in range(4):
        for half, gather in enumerate((b1, b2)):
            for index, source in enumerate(gather.relay_second(which)):
                b_swap(half, 3 + which * 3 + index, source, False).start()
    for which in range(4):
        for gather in (u1, u2):
            gather.forward(which)
    for which in range(1, 4):
        source = me.col(-STEP[which - 1], 0)
        c_out(which - 1)(source).wait_recv()
        c_swap(which)(source).start()
    for half, gather in enumerate((b1, b2)):
        for which in range(4):
            source = gather.finish(which)
            b_swap(half, 5 + which * 3, source, False).start()

    def b_arrived(half, gather):
        for which in range(4):
            if which:
                source = gather.number(SHIFT[which], 0)
                b_swap(half, which - 1, source, True).wait_recv()
            for index, shift in enumerate((-1, 1, 2)):
                source = gather.number(SHIFT[which], shift)
                b_swap(half, 3 + which * 3 + index, source, True).wait_recv()

    def u_relay(which):
        for gather in (u1, u2):
            gather.relay_second(which)

    row_tile = (lax.broadcasted_iota(jnp.int32, (512, 1), 0) // 256) * 16 + me.r
    in1 = (row_tile == pivots[0]) | (row_tile == pivots[1])
    in2 = (row_tile == pivots[2]) | (row_tile == pivots[3])

    def b_part(rows, cols):
        return jnp.concatenate(
            [bg[2 * cols + j, pl.ds(2 * rows, 2)].reshape(512, 256) for j in range(2)], axis=1
        )

    def c_part(cols):
        return jnp.concatenate([cg[:, 2 * cols + j].reshape(512, 256) for j in range(2)], axis=1)

    b_arrived(0, b1)
    block[...] = b_part(0, 0)
    invert(block, block_high, block_low, x1)
    u_relay(0)
    b_arrived(1, b2)
    x1_halves = split(x1[...])
    b12 = split(b_part(0, 1))
    t_halves = split(dot3(split(b_part(1, 0)), x1_halves))
    block[...] = b_part(1, 1) - dot3(t_halves, b12)
    u_relay(1)
    own_c.wait()
    for which in range(4):
        c_swap(which)(me.col(-STEP[which - 1] if which else 0, 1)).wait_recv()
    lower = dot3(split(c_part(0)), x1_halves)
    l1[...] = lower
    lower = jnp.where(in1, 0.0, lower)
    c2[...] = c_part(1) - dot3(split(lower), b12)
    u_relay(2)
    u_relay(3)
    invert(block, block_high, block_low, x2)
    lower2 = dot3(split(c2[...]), split(x2[...]))
    l2[...] = lower2
    lower2 = jnp.where(in1 | in2, 0.0, lower2)
    halves = split(lower2)
    lt_high[:, 512:], lt_low[:, 512:] = halves
    lt_high[:, :512], lt_low[:, :512] = split(lower - dot3(halves, t_halves))

    own_u.wait()
    for which in range(4):
        for gather in (u1, u2):
            gather.finish(which)
    for b in range(4):
        update = dot3((lt_high[...], lt_low[...]), split(ug[b].reshape(1024, 256)))
        col_tile = b * 8 + me.c
        new = m[:, b].reshape(512, 256) - update
        for j in range(4):
            window = slice(j % 2 * 256, j % 2 * 256 + 256)
            if j < 2:
                column = jnp.where(in1, cg[:, j].reshape(512, 256), l1[:, window])
            else:
                column = jnp.where(in1 | in2, c2[:, window], l2[:, window])
            new = jnp.where(col_tile == pivots[j], column, new)
        for half in range(2):
            result[pl.ds(2 * b + half, 512, stride=8), :] = new[:, half * 128 : half * 128 + 128]

    written = [
        pltpu.make_async_copy(result.at[pl.ds(512 * i, 512)], out.at[pl.ds(512 * i, 512)], out_sem.at[i])
        for i in range(8)
    ]
    for copy in written:
        copy.start()
    children.drain()
    for index in range(15):
        row_spread(index)(me.r).wait_send()
    for index in range(7):
        col_spread(index)(me.c).wait_send()
        b_scatter(index)(me.c).wait_send()
        b_gather(index)(me.c).wait_send()
    for index in range(3):
        c_out(index)(me.c).wait_send()
    for which in range(4):
        c_swap(which)(me.c).wait_send()
    for gather in (u1, u2, b1, b2):
        gather.drain()
    for half in range(2):
        for slot in range(15):
            b_swap(half, slot, me.r, False).wait_send()
    for copy in written:
        copy.wait()


def eliminate(panel, targets, front, tiles):
    plane = [DMA((4,)), DMA((4,)), DMA((16,)), DMA((16,))]
    square = pltpu.VMEM((512, 512), F32)
    narrow = pltpu.VMEM((512, 512), BF16)
    return pl.pallas_call(
        pivot_kernel,
        name="pivots",
        out_shape=[
            jax.ShapeDtypeStruct((4096, 128), F32),
            jax.ShapeDtypeStruct((16, 8, 128), jnp.int32),
        ],
        in_specs=[SMEM, VMEM, ANY, ANY],
        out_specs=[ANY] * 2,
        scratch_shapes=[
            pltpu.VMEM((16, 256, 256), F32),
            pltpu.VMEM((8, 128), jnp.int32),
            pltpu.VMEM((16, 256, 256), F32),
            pltpu.VMEM((16, 8, 128), jnp.int32),
            pltpu.VMEM((2, 4, 256, 256), F32),
            pltpu.VMEM((4096, 128), F32),
            pltpu.VMEM((4096, 128), F32),
            pltpu.VMEM((16, 2, 4, 16, 256), F32),
            pltpu.VMEM((8, 4, 64, 256), F32),
            pltpu.VMEM((4, 4, 16, 16, 256), F32),
            pltpu.VMEM((4, 4, 16, 16, 256), F32),
            pltpu.VMEM((8, 4, 64, 256), F32),
            pltpu.VMEM((4, 4, 16, 256), F32),
            pltpu.VMEM((4, 64, 256), F32),
            pltpu.VMEM((8, 4, 8, 256), F32),
            pltpu.VMEM((4, 8, 256), F32),
            square, narrow, narrow, square, square, square, square, square,
            pltpu.VMEM((512, 1024), BF16), pltpu.VMEM((512, 1024), BF16),
            DMA((7,)),
            DMA((15,)), DMA((15,)), DMA((7,)), DMA((7,)),
            DMA((7,)), DMA((7,)), DMA((7,)), DMA((7,)),
            DMA((3,)), DMA((3,)), DMA((4,)), DMA((4,)),
            plane, plane, plane, plane,
            DMA((2, 15)), DMA((2, 15)),
            DMA((8,)), [DMA((2,)), DMA((2,))] + [DMA((16,))] * 8,
        ],
        compiler_params=pltpu.CompilerParams(
            collective_id=0, has_side_effects=True, vmem_limit_bytes=56 * 2**20
        ),
    )(panel, targets, front, tiles)[0]


def hand_over_kernel(source, out, held, sems):
    def copies(step):
        refs = ((source, held), (held, out))[step]
        for i in range(8):
            part = pl.ds(4096 // 8 * i, 4096 // 8)
            yield pltpu.make_async_copy(refs[0].at[part], refs[1].at[part], sems.at[step, i])

    for copy in copies(0):
        copy.start()
    for brought, written in zip(copies(0), copies(1)):
        brought.wait()
        written.start()
    for copy in copies(1):
        copy.wait()


def hand_over(result):
    return pl.pallas_call(
        hand_over_kernel,
        name="hand_over",
        out_shape=jax.ShapeDtypeStruct(result.shape, result.dtype),
        in_specs=[ANY],
        out_specs=ANY,
        scratch_shapes=[pltpu.VMEM(result.shape, result.dtype), DMA((2, 8))],
        compiler_params=pltpu.CompilerParams(vmem_limit_bytes=60 * 2**20),
    )(result)


def shards(front_tiles, child_tiles, child_target, panel_tiles):
    result = eliminate(
        panel_tiles,
        child_target.reshape(16, 2).T,
        front_tiles.reshape(4096, 128),
        child_tiles.reshape(16, 256, 256),
    )
    return hand_over(result).reshape(front_tiles.shape)


def solution(mesh):
    in_specs = (
        P(None, "row", None, None, "col", None),
        P("row", "col", None, None, None),
        P("row", "col", None, None),
        P(),
    )
    out_specs = P(None, "row", None, None, "col", None)
    return jax.shard_map(shards, mesh=mesh, in_specs=in_specs, out_specs=out_specs, check_vma=False)
```

```python
import jax
import jax.numpy as jnp
from jax import lax
from jax.experimental import pallas as pl
from jax.experimental.pallas import tpu as pltpu
from jax.sharding import PartitionSpec as P

MESH = pl.DeviceIdType.MESH
DMA = pltpu.SemaphoreType.DMA
ANY = pl.BlockSpec(memory_space=pl.ANY)
VMEM = pl.BlockSpec(memory_space=pltpu.VMEM)
SMEM = pl.BlockSpec(memory_space=pltpu.SMEM)
F32 = jnp.float32
BF16 = jnp.bfloat16

SQUARE = tuple((a, (a + s) % 4) for s in (1, 3, 0, 2) for a in (1, 3, 0, 2) if (a, s) != (0, 0))
PLANE = (
    (0, 1), (1, 0), (0, 3), (3, 0), (1, 1), (3, 3), (1, 3), (3, 1),
    (0, 2), (2, 0), (1, 2), (2, 1), (3, 2), (2, 3), (2, 2),
)
COLUMN = ((0, 1), (1, 0), (3, 0), (1, 1), (3, 1), (2, 0), (2, 1))
STEP = (1, 3, 2)
SHIFT = (0, -1, 1, 2)
WINDOW = 6
LOOSE_STEPS = 3


class Place:
    def __init__(self):
        self.r = lax.axis_index("row")
        self.c = lax.axis_index("col")
        self.z, self.x = self.r // 4, self.r % 4
        self.y, self.k = self.c // 2, self.c % 2

    def row(self, dz, dx):
        return (self.z + dz + 4) % 4 * 4 + (self.x + dx + 4) % 4

    def col(self, dy, dk):
        return (self.y + dy + 4) % 4 * 2 + (self.k + dk + 2) % 2


def remote(src, dst, send, recv, device):
    return pltpu.make_async_remote_copy(
        src_ref=src, dst_ref=dst, send_sem=send, recv_sem=recv, device_id=device, device_id_type=MESH
    )


def greet(me):
    barrier = pltpu.get_barrier_semaphore()
    for dz, dx in PLANE:
        pl.semaphore_signal(barrier, inc=1, device_id=(me.row(dz, dx), me.c), device_id_type=MESH)
    for dy, dk in COLUMN:
        pl.semaphore_signal(barrier, inc=1, device_id=(me.r, me.col(dy, dk)), device_id_type=MESH)
    pl.semaphore_wait(barrier, len(PLANE) + len(COLUMN))


class Children:
    def __init__(self, me, tiles, spots, mid, mid_spots, landed, landed_spots, sems):
        self.me, self.tiles, self.spots = me, tiles, spots
        self.mid, self.mid_spots, self.landed, self.landed_spots = mid, mid_spots, landed, landed_spots
        (
            self.own, self.own_spot, self.send1, self.recv1, self.spot_send1, self.spot_recv1,
            self.send2, self.recv2, self.spot_send2, self.spot_recv2,
        ) = sems

    def first(self, index):
        target = self.me.row(*SQUARE[index])
        device = (target, self.me.c)
        r = self.me.r
        return (
            remote(self.tiles.at[target], self.mid.at[r], self.send1.at[index], self.recv1.at[index], device),
            remote(
                self.spots, self.mid_spots.at[r], self.spot_send1.at[index], self.spot_recv1.at[index], device
            ),
        )

    def source(self, index):
        if index == len(SQUARE):
            return self.me.r, self.tiles.at[self.me.r], self.spots
        dz, dx = SQUARE[index]
        source = self.me.row(-dz, -dx)
        return source, self.mid.at[source], self.mid_spots.at[source]

    def _second(self, index, away):
        source, tile, spot = self.source(index)
        half = source // 8
        place = half * 8 + self.me.c
        if not away:
            return (
                pltpu.make_async_copy(tile, self.landed.at[place], self.own.at[half]),
                pltpu.make_async_copy(spot, self.landed_spots.at[place], self.own_spot.at[half]),
            )
        device = (self.me.r, source % 8)
        return (
            remote(tile, self.landed.at[place], self.send2.at[index], self.recv2.at[place], device),
            remote(
                spot, self.landed_spots.at[place], self.spot_send2.at[index], self.spot_recv2.at[place], device
            ),
        )

    def pass_on(self, index):
        if index < len(SQUARE):
            for copy in self.first(index):
                copy.wait_recv()
        col = self.source(index)[0] % 8

        @pl.when(col == self.me.c)
        def _():
            for copy in self._second(index, False):
                copy.start()

        @pl.when(col != self.me.c)
        def _():
            for copy in self._second(index, True):
                copy.start()

    def send(self):
        last = len(SQUARE)
        for index in range(last):
            if index == WINDOW:
                self.pass_on(last)
            if index >= WINDOW:
                self.pass_on(index - WINDOW)
            for copy in self.first(index):
                copy.start()
        for index in range(last - WINDOW, last):
            self.pass_on(index)

    def first_half(self):
        def rank(value):
            return jnp.where(value == 1, 0, jnp.where(value == 3, 1, jnp.where(value == 0, 2, 3)))

        steps = []
        for half in range(2):
            source = self.me.c + 8 * half
            dz, dx = (self.me.z - source // 4 + 4) % 4, (self.me.x - source % 4 + 4) % 4
            step = 4 * rank((dx - dz + 4) % 4) + rank(dz)
            steps.append(jnp.where(source == self.me.r, -1, step))
        return jnp.where(steps[0] < steps[1], 0, 1)

    def arrive(self, half, dy, dk):
        place = half * 8 + self.me.col(dy, dk)
        tile, spot = self.landed.at[place], self.landed_spots.at[place]
        if (dy, dk) == (0, 0):
            pltpu.make_async_copy(tile, tile, self.own.at[half]).wait()
            pltpu.make_async_copy(spot, spot, self.own_spot.at[half]).wait()
        else:
            device = (self.me.r, self.me.c)
            remote(tile, tile, self.send2.at[0], self.recv2.at[place], device).wait_recv()
            remote(spot, spot, self.spot_send2.at[0], self.spot_recv2.at[place], device).wait_recv()
        return place

    def drain(self):
        for index in range(len(SQUARE) + 1):
            if index < len(SQUARE):
                for copy in self.first(index):
                    copy.wait_send()
            col = self.source(index)[0] % 8

            @pl.when(col != self.me.c)
            def _(index=index):
                for copy in self._second(index, True):
                    copy.wait_send()


class PlaneGather:
    def __init__(self, me, at, own, x_first, relayed, sems):
        self.me, self.at, self.own, self.x_first = me, at, own, x_first
        self.send1, self.recv1, self.send2, self.recv2 = sems
        self.relayed = relayed
        self.near = range(2 if relayed else 3)
        self.far = (2, 3) if relayed else (2,)

    def number(self, one, two):
        return self.me.row(two, one) if self.x_first else self.me.row(one, two)

    def _copy(self, index, own, source, landed, send, recv, targets):
        block, landed = self.at(source) if own is None else own, self.at(landed)
        if self.relayed and index >= 2:
            half = pl.ds(2 * (index - 2), 2)
            block, landed = self.at(source).at[half], landed.at[half]
            index -= 2
        return remote(block, landed, send, recv, (targets[index], self.me.c))

    def _first(self, index, source, landed):
        targets = [self.number(step, 0) for step in (1, -1, 2)]
        return self._copy(
            index, self.own, source, landed, self.send1.at[index], self.recv1.at[index], targets
        )

    def _second(self, which, index, source, landed):
        targets = [self.number(0, step) for step in (1, -1, 2)]
        slot = which * 4 + index
        return self._copy(
            index, None if which else self.own, source, landed,
            self.send2.at[slot], self.recv2.at[slot], targets,
        )

    def start(self):
        for index in self.near:
            self._first(index, self.me.r, self.me.r).start()

    def relay(self):
        for index, shift in enumerate((-1, 1)):
            source = self.number(shift, 0)
            self._first(index, self.me.r, source).wait_recv()
            if self.relayed:
                self._first(index + 2, source, source).start()

    def forward(self, which):
        source = self.number(SHIFT[which], 0)
        if which == 3:
            for index in self.far:
                self._first(index, source, source).wait_recv()
        for index in self.near:
            self._second(which, index, source, source).start()
        return source

    def relay_second(self, which):
        landed = []
        for index, shift in enumerate((-1, 1)):
            source = self.number(SHIFT[which], shift)
            self._second(which, index, source, source).wait_recv()
            if self.relayed:
                self._second(which, index + 2, source, source).start()
            landed.append(source)
        return landed

    def finish(self, which):
        source = self.number(SHIFT[which], 2)
        for index in self.far:
            self._second(which, index, source, source).wait_recv()
        return source

    def drain(self):
        messages = (*range(2), *self.far)
        for index in messages:
            self._first(index, self.me.r, self.me.r).wait_send()
        for which in range(4):
            for index in messages:
                self._second(which, index, self.me.r, self.me.r).wait_send()


def split(value):
    high = value.astype(BF16)
    return high, (value - high.astype(F32)).astype(BF16)


def dot1(a, b):
    return jnp.dot(a, b, preferred_element_type=F32)


def dot3(a, b):
    return dot1(a[0], b[0]) + (dot1(a[0], b[1]) + dot1(a[1], b[0]))


def invert(block, block_high, block_low, estimate):
    size = block.shape[0]
    diagonal = lax.broadcasted_iota(jnp.int32, (size, size), 0) == lax.broadcasted_iota(
        jnp.int32, (size, size), 1
    )
    value = block[...]
    block_high[...], block_low[...] = split(value)
    weights = jnp.where(diagonal, value, 0.0)
    by_row = 1.0 / jnp.sum(weights, axis=1, keepdims=True)
    by_col = 1.0 / jnp.sum(weights, axis=0, keepdims=True)
    estimate[...] = jnp.where(diagonal, by_col, -(by_row * value * by_col))

    def loose(step, carry):
        now = estimate[...]
        high = now.astype(BF16)
        product = dot1(block_high[...], high)
        estimate[...] = 2.0 * now - dot1(high, product.astype(BF16))
        return carry

    def residual(halves):
        return jnp.where(diagonal, 1.0, 0.0) - dot3((block_high[...], block_low[...]), halves)

    lax.fori_loop(0, LOOSE_STEPS, loose, 0)
    now = estimate[...]
    halves = split(now)
    estimate[...] = now + dot1(halves[0], residual(halves).astype(BF16))
    now = estimate[...]
    halves = split(now)
    estimate[...] = now + dot3(halves, split(residual(halves)))


def pivot_kernel(
    panel, targets, front_in, tiles, out, mid_spots, mid, spots, landed, landed_spots, m, front, result, rows, cols, ug, bg, cg, upc, cpc, bsc, bpc,
    block, block_high, block_low, x1, x2, l1, l2, c2, lt_high, lt_low, own,
    row_s, row_r, col_s, col_r, bs_s, bs_r, bc_s, bc_r, c_s, c_r, cx_s, cx_r, ua, ub, ba, bb, bx_s, bx_r,
    out_sem, child_sems,
):
    me = Place()
    greet(me)
    pivots = [panel[j // 2, j % 2] for j in range(4)]

    spots[...] = jnp.zeros_like(spots)
    spots[0:1, 0:16] = targets[0:1, :] // 16 * 4 + targets[1:2, :] // 8
    children = Children(me, tiles, spots, mid, mid_spots, landed, landed_spots, child_sems)
    brought = [
        pltpu.make_async_copy(front_in.at[pl.ds(512 * i, 512)], front.at[pl.ds(512 * i, 512)], out_sem.at[i])
        for i in range(8)
    ]
    children.send()
    for copy in brought:
        copy.start()
    for copy in brought:
        copy.wait()
    for chunk in range(8):
        part = front[pl.ds(chunk, 512, stride=8), :].reshape(2, 256, 128)
        m[:, chunk // 2, :, pl.ds(chunk % 2 * 128, 128)] = part
    lane = lax.broadcasted_iota(jnp.int32, (8, 128), 1)
    first_half = children.first_half()
    for half in (first_half, 1 - first_half):
        for group in (((0, 0), *COLUMN[:3]), COLUMN[3:]):
            places = [children.arrive(half, dy, dk) for dy, dk in group]
            spot = []
            for place in places:
                mine = jnp.where(lane == me.r, landed_spots[place], 0)
                spot.append(jnp.sum(mine.astype(F32), keepdims=True).astype(jnp.int32))

            def add(slot, carry, places=places, spot=spot):
                parts = [jnp.where(s == slot, landed[p], 0.0) for s, p in zip(spot, places)]
                m[slot // 4, slot % 4] += (parts[0] + parts[1]) + (parts[2] + parts[3])
                return carry

            lax.fori_loop(0, 8, add, 0)

    def row_slice(target):
        return m.at[:, :, pl.ds(pl.multiple_of(target * 16, 16), 16), :]

    def col_slice(target):
        return m.at[target // 4, :, pl.ds(pl.multiple_of(target % 4 * 64, 64), 64), :]

    def row_spread(index):
        target = me.row(*PLANE[index])
        return lambda source: remote(
            row_slice(target), rows.at[source], row_s.at[index], row_r.at[index], (target, me.c)
        )

    def col_spread(index):
        target = me.col(*COLUMN[index])
        return lambda source: remote(
            col_slice(target), cols.at[source], col_s.at[index], col_r.at[index], (me.r, target)
        )

    for index in range(15):
        row_spread(index)(me.r).start()
        if index < 7:
            col_spread(index)(me.c).start()
    mine = (
        pltpu.make_async_copy(row_slice(me.r), rows.at[me.r], own.at[0]),
        pltpu.make_async_copy(col_slice(me.c), cols.at[me.c], own.at[1]),
    )
    for copy in mine:
        copy.start()
    for copy in mine:
        copy.wait()
    for index, (dz, dx) in enumerate(PLANE):
        row_spread(index)(me.row(-dz, -dx)).wait_recv()
    for j, pivot in enumerate(pivots):
        upc[:, j] = rows[pivot % 16, pivot // 16]

    def b_rows(col):
        return upc.at[:, col // 2, pl.ds(pl.multiple_of(col % 2 * 8, 8), 8), :]

    def b_scatter(index):
        target = me.col(*COLUMN[index])
        return lambda source: remote(
            b_rows(target), bsc.at[source], bs_s.at[index], bs_r.at[index], (me.r, target)
        )

    for index in range(7):
        b_scatter(index)(me.c).start()
    own_scatter = pltpu.make_async_copy(b_rows(me.c), bsc.at[me.c], own.at[2])
    own_scatter.start()

    def u_at(first):
        return lambda source: ug.at[:, pl.ds(first, 2), source]

    u1 = PlaneGather(me, u_at(0), upc.at[:, pl.ds(0, 2)], True, True, ua)
    u2 = PlaneGather(me, u_at(2), upc.at[:, pl.ds(2, 2)], False, True, ub)
    u1.start()
    u2.start()
    own_u = pltpu.make_async_copy(upc, ug.at[:, :, me.r], own.at[3])
    own_u.start()

    own_scatter.wait()
    for index, (dy, dk) in enumerate(COLUMN):
        b_scatter(index)(me.col(-dy, -dk)).wait_recv()
    for j, pivot in enumerate(pivots):
        bpc[j] = bsc[pivot % 8, pivot // 8]

    def b_piece(col):
        return bg.at[:, col // 2, me.r, pl.ds(pl.multiple_of(col % 2 * 8, 8), 8), :]

    def b_gather(index):
        return lambda source: remote(
            bpc, b_piece(source), bc_s.at[index], bc_r.at[index], (me.r, me.col(*COLUMN[index]))
        )

    for index in range(7):
        b_gather(index)(me.c).start()
    own_b = pltpu.make_async_copy(bpc, b_piece(me.c), own.at[4])
    own_b.start()

    for index, (dy, dk) in enumerate(COLUMN):
        col_spread(index)(me.col(-dy, -dk)).wait_recv()
    for j, pivot in enumerate(pivots):
        cpc[j] = cols[pivot % 8, pivot // 8]

    def c_out(index):
        return lambda source: remote(
            cpc, cg.at[source], c_s.at[index], c_r.at[index], (me.r, me.col(STEP[index], 0))
        )

    def c_swap(which):
        source = me.col(-STEP[which - 1] if which else 0, 0)
        src = cg.at[source] if which else cpc
        return lambda landed: remote(
            src, cg.at[landed], cx_s.at[which], cx_r.at[which], (me.r, me.col(0, 1))
        )

    own_b.wait()
    for index, (dy, dk) in enumerate(COLUMN):
        b_gather(index)(me.col(-dy, -dk)).wait_recv()

    def b_at(pivot):
        return lambda source: bg.at[:, pivot, source]

    b1 = PlaneGather(me, b_at(me.k), b_at(me.k)(me.r), True, True, ba)
    b2 = PlaneGather(me, b_at(2 + me.k), b_at(2 + me.k)(me.r), False, True, bb)
    b1.start()
    b2.start()

    def b_swap(half, slot, source, back):
        pivot = 2 * half + (1 - me.k if back else me.k)
        block = bg.at[:, pivot, source]
        return remote(block, block, bx_s.at[half, slot], bx_r.at[half, slot], (me.r, me.col(0, 1)))

    for gather in (b1, b2):
        gather.forward(0)
    for index in range(3):
        c_out(index)(me.c).start()
    c_swap(0)(me.c).start()
    own_c = pltpu.make_async_copy(cpc, cg.at[me.c], own.at[5])
    own_c.start()

    for gather in (b1, b2):
        gather.relay()
    for which in range(1, 4):
        for half, gather in enumerate((b1, b2)):
            source = gather.forward(which)
            b_swap(half, which - 1, source, False).start()
    for gather in (u1, u2):
        gather.relay()
    for which in range(4):
        for half, gather in enumerate((b1, b2)):
            for index, source in enumerate(gather.relay_second(which)):
                b_swap(half, 3 + which * 3 + index, source, False).start()
    for which in range(4):
        for gather in (u1, u2):
            gather.forward(which)
    for which in range(1, 4):
        source = me.col(-STEP[which - 1], 0)
        c_out(which - 1)(source).wait_recv()
        c_swap(which)(source).start()
    for half, gather in enumerate((b1, b2)):
        for which in range(4):
            source = gather.finish(which)
            b_swap(half, 5 + which * 3, source, False).start()

    def b_arrived(half, gather):
        for which in range(4):
            if which:
                source = gather.number(SHIFT[which], 0)
                b_swap(half, which - 1, source, True).wait_recv()
            for index, shift in enumerate((-1, 1, 2)):
                source = gather.number(SHIFT[which], shift)
                b_swap(half, 3 + which * 3 + index, source, True).wait_recv()

    def u_relay(which):
        for gather in (u1, u2):
            gather.relay_second(which)

    row_tile = (lax.broadcasted_iota(jnp.int32, (512, 1), 0) // 256) * 16 + me.r
    in1 = (row_tile == pivots[0]) | (row_tile == pivots[1])
    in2 = (row_tile == pivots[2]) | (row_tile == pivots[3])

    def b_part(rows, cols):
        return jnp.concatenate(
            [bg[2 * cols + j, pl.ds(2 * rows, 2)].reshape(512, 256) for j in range(2)], axis=1
        )

    def c_part(cols):
        return jnp.concatenate([cg[:, 2 * cols + j].reshape(512, 256) for j in range(2)], axis=1)

    b_arrived(0, b1)
    block[...] = b_part(0, 0)
    invert(block, block_high, block_low, x1)
    u_relay(0)
    b_arrived(1, b2)
    x1_halves = split(x1[...])
    b12 = split(b_part(0, 1))
    t_halves = split(dot3(split(b_part(1, 0)), x1_halves))
    block[...] = b_part(1, 1) - dot3(t_halves, b12)
    u_relay(1)
    own_c.wait()
    for which in range(4):
        c_swap(which)(me.col(-STEP[which - 1] if which else 0, 1)).wait_recv()
    lower = dot3(split(c_part(0)), x1_halves)
    l1[...] = lower
    lower = jnp.where(in1, 0.0, lower)
    c2[...] = c_part(1) - dot3(split(lower), b12)
    u_relay(2)
    u_relay(3)
    invert(block, block_high, block_low, x2)
    lower2 = dot3(split(c2[...]), split(x2[...]))
    l2[...] = lower2
    lower2 = jnp.where(in1 | in2, 0.0, lower2)
    halves = split(lower2)
    lt_high[:, 512:], lt_low[:, 512:] = halves
    lt_high[:, :512], lt_low[:, :512] = split(lower - dot3(halves, t_halves))

    own_u.wait()
    for which in range(4):
        for gather in (u1, u2):
            gather.finish(which)
    for b in range(4):
        update = dot3((lt_high[...], lt_low[...]), split(ug[b].reshape(1024, 256)))
        col_tile = b * 8 + me.c
        new = m[:, b].reshape(512, 256) - update
        for j in range(4):
            window = slice(j % 2 * 256, j % 2 * 256 + 256)
            if j < 2:
                column = jnp.where(in1, cg[:, j].reshape(512, 256), l1[:, window])
            else:
                column = jnp.where(in1 | in2, c2[:, window], l2[:, window])
            new = jnp.where(col_tile == pivots[j], column, new)
        for half in range(2):
            result[pl.ds(2 * b + half, 512, stride=8), :] = new[:, half * 128 : half * 128 + 128]

    written = [
        pltpu.make_async_copy(result.at[pl.ds(512 * i, 512)], out.at[pl.ds(512 * i, 512)], out_sem.at[i])
        for i in range(8)
    ]
    for copy in written:
        copy.start()
    children.drain()
    for index in range(15):
        row_spread(index)(me.r).wait_send()
    for index in range(7):
        col_spread(index)(me.c).wait_send()
        b_scatter(index)(me.c).wait_send()
        b_gather(index)(me.c).wait_send()
    for index in range(3):
        c_out(index)(me.c).wait_send()
    for which in range(4):
        c_swap(which)(me.c).wait_send()
    for gather in (u1, u2, b1, b2):
        gather.drain()
    for half in range(2):
        for slot in range(15):
            b_swap(half, slot, me.r, False).wait_send()
    for copy in written:
        copy.wait()


def eliminate(panel, targets, front, tiles):
    plane = [DMA((4,)), DMA((4,)), DMA((16,)), DMA((16,))]
    square = pltpu.VMEM((512, 512), F32)
    narrow = pltpu.VMEM((512, 512), BF16)
    return pl.pallas_call(
        pivot_kernel,
        name="pivots",
        out_shape=[
            jax.ShapeDtypeStruct((4096, 128), F32),
            jax.ShapeDtypeStruct((16, 8, 128), jnp.int32),
        ],
        in_specs=[SMEM, VMEM, ANY, ANY],
        out_specs=[ANY] * 2,
        scratch_shapes=[
            pltpu.VMEM((16, 256, 256), F32),
            pltpu.VMEM((8, 128), jnp.int32),
            pltpu.VMEM((16, 256, 256), F32),
            pltpu.VMEM((16, 8, 128), jnp.int32),
            pltpu.VMEM((2, 4, 256, 256), F32),
            pltpu.VMEM((4096, 128), F32),
            pltpu.VMEM((4096, 128), F32),
            pltpu.VMEM((16, 2, 4, 16, 256), F32),
            pltpu.VMEM((8, 4, 64, 256), F32),
            pltpu.VMEM((4, 4, 16, 16, 256), F32),
            pltpu.VMEM((4, 4, 16, 16, 256), F32),
            pltpu.VMEM((8, 4, 64, 256), F32),
            pltpu.VMEM((4, 4, 16, 256), F32),
            pltpu.VMEM((4, 64, 256), F32),
            pltpu.VMEM((8, 4, 8, 256), F32),
            pltpu.VMEM((4, 8, 256), F32),
            square, narrow, narrow, square, square, square, square, square,
            pltpu.VMEM((512, 1024), BF16), pltpu.VMEM((512, 1024), BF16),
            DMA((7,)),
            DMA((15,)), DMA((15,)), DMA((7,)), DMA((7,)),
            DMA((7,)), DMA((7,)), DMA((7,)), DMA((7,)),
            DMA((3,)), DMA((3,)), DMA((4,)), DMA((4,)),
            plane, plane, plane, plane,
            DMA((2, 15)), DMA((2, 15)),
            DMA((8,)), [DMA((2,)), DMA((2,))] + [DMA((16,))] * 8,
        ],
        compiler_params=pltpu.CompilerParams(
            collective_id=0, has_side_effects=True, vmem_limit_bytes=56 * 2**20
        ),
    )(panel, targets, front, tiles)[0]


def hand_over_kernel(source, out, held, sems):
    def copies(step):
        refs = ((source, held), (held, out))[step]
        for i in range(8):
            part = pl.ds(4096 // 8 * i, 4096 // 8)
            yield pltpu.make_async_copy(refs[0].at[part], refs[1].at[part], sems.at[step, i])

    for copy in copies(0):
        copy.start()
    for brought, written in zip(copies(0), copies(1)):
        brought.wait()
        written.start()
    for copy in copies(1):
        copy.wait()


def hand_over(result):
    return pl.pallas_call(
        hand_over_kernel,
        name="hand_over",
        out_shape=jax.ShapeDtypeStruct(result.shape, result.dtype),
        in_specs=[ANY],
        out_specs=ANY,
        scratch_shapes=[pltpu.VMEM(result.shape, result.dtype), DMA((2, 8))],
        compiler_params=pltpu.CompilerParams(vmem_limit_bytes=60 * 2**20),
    )(result)


def shards(front_tiles, child_tiles, child_target, panel_tiles):
    result = eliminate(
        panel_tiles,
        child_target.reshape(16, 2).T,
        front_tiles.reshape(4096, 128),
        child_tiles.reshape(16, 256, 256),
    )
    return hand_over(result).reshape(front_tiles.shape)


def solution(mesh):
    in_specs = (
        P(None, "row", None, None, "col", None),
        P("row", "col", None, None, None),
        P("row", "col", None, None),
        P(),
    )
    out_specs = P(None, "row", None, None, "col", None)
    return jax.shard_map(shards, mesh=mesh, in_specs=in_specs, out_specs=out_specs, check_vma=False)
```

```python
import jax
import jax.numpy as jnp
from jax import lax
from jax.experimental import pallas as pl
from jax.experimental.pallas import tpu as pltpu
from jax.sharding import PartitionSpec as P

MESH = pl.DeviceIdType.MESH
DMA = pltpu.SemaphoreType.DMA
ANY = pl.BlockSpec(memory_space=pl.ANY)
VMEM = pl.BlockSpec(memory_space=pltpu.VMEM)
SMEM = pl.BlockSpec(memory_space=pltpu.SMEM)
F32 = jnp.float32
BF16 = jnp.bfloat16

SQUARE = tuple((a, (a + s) % 4) for s in (1, 3, 0, 2) for a in (1, 3, 0, 2) if (a, s) != (0, 0))
PLANE = (
    (0, 1), (1, 0), (0, 3), (3, 0), (1, 1), (3, 3), (1, 3), (3, 1),
    (0, 2), (2, 0), (1, 2), (2, 1), (3, 2), (2, 3), (2, 2),
)
COLUMN = ((0, 1), (1, 0), (3, 0), (1, 1), (3, 1), (2, 0), (2, 1))
STEP = (1, 3, 2)
SHIFT = (0, -1, 1, 2)
WINDOW = 6
LOOSE_STEPS = 3


class Place:
    def __init__(self):
        self.r = lax.axis_index("row")
        self.c = lax.axis_index("col")
        self.z, self.x = self.r // 4, self.r % 4
        self.y, self.k = self.c // 2, self.c % 2

    def row(self, dz, dx):
        return (self.z + dz + 4) % 4 * 4 + (self.x + dx + 4) % 4

    def col(self, dy, dk):
        return (self.y + dy + 4) % 4 * 2 + (self.k + dk + 2) % 2


def remote(src, dst, send, recv, device):
    return pltpu.make_async_remote_copy(
        src_ref=src, dst_ref=dst, send_sem=send, recv_sem=recv, device_id=device, device_id_type=MESH
    )


def greet(me):
    barrier = pltpu.get_barrier_semaphore()
    for dz, dx in PLANE:
        pl.semaphore_signal(barrier, inc=1, device_id=(me.row(dz, dx), me.c), device_id_type=MESH)
    for dy, dk in COLUMN:
        pl.semaphore_signal(barrier, inc=1, device_id=(me.r, me.col(dy, dk)), device_id_type=MESH)
    pl.semaphore_wait(barrier, len(PLANE) + len(COLUMN))


class Children:
    def __init__(self, me, tiles, spots, mid, mid_spots, landed, landed_spots, sems):
        self.me, self.tiles, self.spots = me, tiles, spots
        self.mid, self.mid_spots, self.landed, self.landed_spots = mid, mid_spots, landed, landed_spots
        (
            self.own, self.own_spot, self.send1, self.recv1, self.spot_send1, self.spot_recv1,
            self.send2, self.recv2, self.spot_send2, self.spot_recv2,
        ) = sems

    def first(self, index):
        target = self.me.row(*SQUARE[index])
        device = (target, self.me.c)
        r = self.me.r
        return (
            remote(self.tiles.at[target], self.mid.at[r], self.send1.at[index], self.recv1.at[index], device),
            remote(
                self.spots, self.mid_spots.at[r], self.spot_send1.at[index], self.spot_recv1.at[index], device
            ),
        )

    def source(self, index):
        if index == len(SQUARE):
            return self.me.r, self.tiles.at[self.me.r], self.spots
        dz, dx = SQUARE[index]
        source = self.me.row(-dz, -dx)
        return source, self.mid.at[source], self.mid_spots.at[source]

    def _second(self, index, away):
        source, tile, spot = self.source(index)
        half = source // 8
        place = half * 8 + self.me.c
        if not away:
            return (
                pltpu.make_async_copy(tile, self.landed.at[place], self.own.at[half]),
                pltpu.make_async_copy(spot, self.landed_spots.at[place], self.own_spot.at[half]),
            )
        device = (self.me.r, source % 8)
        return (
            remote(tile, self.landed.at[place], self.send2.at[index], self.recv2.at[place], device),
            remote(
                spot, self.landed_spots.at[place], self.spot_send2.at[index], self.spot_recv2.at[place], device
            ),
        )

    def pass_on(self, index):
        if index < len(SQUARE):
            for copy in self.first(index):
                copy.wait_recv()
        col = self.source(index)[0] % 8

        @pl.when(col == self.me.c)
        def _():
            for copy in self._second(index, False):
                copy.start()

        @pl.when(col != self.me.c)
        def _():
            for copy in self._second(index, True):
                copy.start()

    def send(self):
        last = len(SQUARE)
        for index in range(last):
            if index == WINDOW:
                self.pass_on(last)
            if index >= WINDOW:
                self.pass_on(index - WINDOW)
            for copy in self.first(index):
                copy.start()
        for index in range(last - WINDOW, last):
            self.pass_on(index)

    def first_half(self):
        def rank(value):
            return jnp.where(value == 1, 0, jnp.where(value == 3, 1, jnp.where(value == 0, 2, 3)))

        steps = []
        for half in range(2):
            source = self.me.c + 8 * half
            dz, dx = (self.me.z - source // 4 + 4) % 4, (self.me.x - source % 4 + 4) % 4
            step = 4 * rank((dx - dz + 4) % 4) + rank(dz)
            steps.append(jnp.where(source == self.me.r, -1, step))
        return jnp.where(steps[0] < steps[1], 0, 1)

    def arrive(self, half, dy, dk):
        place = half * 8 + self.me.col(dy, dk)
        tile, spot = self.landed.at[place], self.landed_spots.at[place]
        if (dy, dk) == (0, 0):
            pltpu.make_async_copy(tile, tile, self.own.at[half]).wait()
            pltpu.make_async_copy(spot, spot, self.own_spot.at[half]).wait()
        else:
            device = (self.me.r, self.me.c)
            remote(tile, tile, self.send2.at[0], self.recv2.at[place], device).wait_recv()
            remote(spot, spot, self.spot_send2.at[0], self.spot_recv2.at[place], device).wait_recv()
        return place

    def drain(self):
        for index in range(len(SQUARE) + 1):
            if index < len(SQUARE):
                for copy in self.first(index):
                    copy.wait_send()
            col = self.source(index)[0] % 8

            @pl.when(col != self.me.c)
            def _(index=index):
                for copy in self._second(index, True):
                    copy.wait_send()


class PlaneGather:
    def __init__(self, me, at, own, x_first, relayed, sems):
        self.me, self.at, self.own, self.x_first = me, at, own, x_first
        self.send1, self.recv1, self.send2, self.recv2 = sems
        self.relayed = relayed
        self.near = range(2 if relayed else 3)
        self.far = (2, 3) if relayed else (2,)

    def number(self, one, two):
        return self.me.row(two, one) if self.x_first else self.me.row(one, two)

    def _copy(self, index, own, source, landed, send, recv, targets):
        block, landed = self.at(source) if own is None else own, self.at(landed)
        if self.relayed and index >= 2:
            half = pl.ds(2 * (index - 2), 2)
            block, landed = self.at(source).at[half], landed.at[half]
            index -= 2
        return remote(block, landed, send, recv, (targets[index], self.me.c))

    def _first(self, index, source, landed):
        targets = [self.number(step, 0) for step in (1, -1, 2)]
        return self._copy(
            index, self.own, source, landed, self.send1.at[index], self.recv1.at[index], targets
        )

    def _second(self, which, index, source, landed):
        targets = [self.number(0, step) for step in (1, -1, 2)]
        slot = which * 4 + index
        return self._copy(
            index, None if which else self.own, source, landed,
            self.send2.at[slot], self.recv2.at[slot], targets,
        )

    def start(self):
        for index in self.near:
            self._first(index, self.me.r, self.me.r).start()

    def relay(self):
        for index, shift in enumerate((-1, 1)):
            source = self.number(shift, 0)
            self._first(index, self.me.r, source).wait_recv()
            if self.relayed:
                self._first(index + 2, source, source).start()

    def forward(self, which):
        source = self.number(SHIFT[which], 0)
        if which == 3:
            for index in self.far:
                self._first(index, source, source).wait_recv()
        for index in self.near:
            self._second(which, index, source, source).start()
        return source

    def relay_second(self, which):
        landed = []
        for index, shift in enumerate((-1, 1)):
            source = self.number(SHIFT[which], shift)
            self._second(which, index, source, source).wait_recv()
            if self.relayed:
                self._second(which, index + 2, source, source).start()
            landed.append(source)
        return landed

    def finish(self, which):
        source = self.number(SHIFT[which], 2)
        for index in self.far:
            self._second(which, index, source, source).wait_recv()
        return source

    def drain(self):
        messages = (*range(2), *self.far)
        for index in messages:
            self._first(index, self.me.r, self.me.r).wait_send()
        for which in range(4):
            for index in messages:
                self._second(which, index, self.me.r, self.me.r).wait_send()


def split(value):
    high = value.astype(BF16)
    return high, (value - high.astype(F32)).astype(BF16)


def dot1(a, b):
    return jnp.dot(a, b, preferred_element_type=F32)


def dot3(a, b):
    return dot1(a[0], b[0]) + (dot1(a[0], b[1]) + dot1(a[1], b[0]))


def invert(block, block_high, block_low, estimate):
    size = block.shape[0]
    diagonal = lax.broadcasted_iota(jnp.int32, (size, size), 0) == lax.broadcasted_iota(
        jnp.int32, (size, size), 1
    )
    value = block[...]
    block_high[...], block_low[...] = split(value)
    weights = jnp.where(diagonal, value, 0.0)
    by_row = 1.0 / jnp.sum(weights, axis=1, keepdims=True)
    by_col = 1.0 / jnp.sum(weights, axis=0, keepdims=True)
    estimate[...] = jnp.where(diagonal, by_col, -(by_row * value * by_col))

    def loose(step, carry):
        now = estimate[...]
        high = now.astype(BF16)
        product = dot1(block_high[...], high)
        estimate[...] = 2.0 * now - dot1(high, product.astype(BF16))
        return carry

    def residual(halves):
        return jnp.where(diagonal, 1.0, 0.0) - dot3((block_high[...], block_low[...]), halves)

    lax.fori_loop(0, LOOSE_STEPS, loose, 0)
    now = estimate[...]
    halves = split(now)
    estimate[...] = now + dot1(halves[0], residual(halves).astype(BF16))
    now = estimate[...]
    halves = split(now)
    estimate[...] = now + dot3(halves, split(residual(halves)))


def pivot_kernel(
    panel, targets, front_in, tiles, out, mid_spots, mid, spots, landed, landed_spots, m, front, result, rows, cols, ug, bg, cg, upc, cpc, bsc, bpc,
    block, block_high, block_low, x1, x2, l1, l2, c2, lt_high, lt_low, own,
    row_s, row_r, col_s, col_r, bs_s, bs_r, bc_s, bc_r, c_s, c_r, cx_s, cx_r, ua, ub, ba, bb, bx_s, bx_r,
    out_sem, child_sems,
):
    me = Place()
    greet(me)
    pivots = [panel[j // 2, j % 2] for j in range(4)]

    spots[...] = jnp.zeros_like(spots)
    spots[0:1, 0:16] = targets[0:1, :] // 16 * 4 + targets[1:2, :] // 8
    children = Children(me, tiles, spots, mid, mid_spots, landed, landed_spots, child_sems)
    brought = [
        pltpu.make_async_copy(front_in.at[pl.ds(512 * i, 512)], front.at[pl.ds(512 * i, 512)], out_sem.at[i])
        for i in range(8)
    ]
    children.send()
    for copy in brought:
        copy.start()
    for copy in brought:
        copy.wait()
    for chunk in range(8):
        part = front[pl.ds(chunk, 512, stride=8), :].reshape(2, 256, 128)
        m[:, chunk // 2, :, pl.ds(chunk % 2 * 128, 128)] = part
    lane = lax.broadcasted_iota(jnp.int32, (8, 128), 1)
    first_half = children.first_half()
    for half in (first_half, 1 - first_half):
        for group in (((0, 0), *COLUMN[:3]), COLUMN[3:]):
            places = [children.arrive(half, dy, dk) for dy, dk in group]
            spot = []
            for place in places:
                mine = jnp.where(lane == me.r, landed_spots[place], 0)
                spot.append(jnp.sum(mine.astype(F32), keepdims=True).astype(jnp.int32))

            def add(slot, carry, places=places, spot=spot):
                parts = [jnp.where(s == slot, landed[p], 0.0) for s, p in zip(spot, places)]
                m[slot // 4, slot % 4] += (parts[0] + parts[1]) + (parts[2] + parts[3])
                return carry

            lax.fori_loop(0, 8, add, 0)

    def row_slice(target):
        return m.at[:, :, pl.ds(pl.multiple_of(target * 16, 16), 16), :]

    def col_slice(target):
        return m.at[target // 4, :, pl.ds(pl.multiple_of(target % 4 * 64, 64), 64), :]

    def row_spread(index):
        target = me.row(*PLANE[index])
        return lambda source: remote(
            row_slice(target), rows.at[source], row_s.at[index], row_r.at[index], (target, me.c)
        )

    def col_spread(index):
        target = me.col(*COLUMN[index])
        return lambda source: remote(
            col_slice(target), cols.at[source], col_s.at[index], col_r.at[index], (me.r, target)
        )

    for index in range(15):
        row_spread(index)(me.r).start()
        if index < 7:
            col_spread(index)(me.c).start()
    mine = (
        pltpu.make_async_copy(row_slice(me.r), rows.at[me.r], own.at[0]),
        pltpu.make_async_copy(col_slice(me.c), cols.at[me.c], own.at[1]),
    )
    for copy in mine:
        copy.start()
    for copy in mine:
        copy.wait()
    for index, (dz, dx) in enumerate(PLANE):
        row_spread(index)(me.row(-dz, -dx)).wait_recv()
    for j, pivot in enumerate(pivots):
        upc[:, j] = rows[pivot % 16, pivot // 16]

    def b_rows(col):
        return upc.at[:, col // 2, pl.ds(pl.multiple_of(col % 2 * 8, 8), 8), :]

    def b_scatter(index):
        target = me.col(*COLUMN[index])
        return lambda source: remote(
            b_rows(target), bsc.at[source], bs_s.at[index], bs_r.at[index], (me.r, target)
        )

    for index in range(7):
        b_scatter(index)(me.c).start()
    own_scatter = pltpu.make_async_copy(b_rows(me.c), bsc.at[me.c], own.at[2])
    own_scatter.start()

    def u_at(first):
        return lambda source: ug.at[:, pl.ds(first, 2), source]

    u1 = PlaneGather(me, u_at(0), upc.at[:, pl.ds(0, 2)], True, True, ua)
    u2 = PlaneGather(me, u_at(2), upc.at[:, pl.ds(2, 2)], False, True, ub)
    u1.start()
    u2.start()
    own_u = pltpu.make_async_copy(upc, ug.at[:, :, me.r], own.at[3])
    own_u.start()

    own_scatter.wait()
    for index, (dy, dk) in enumerate(COLUMN):
        b_scatter(index)(me.col(-dy, -dk)).wait_recv()
    for j, pivot in enumerate(pivots):
        bpc[j] = bsc[pivot % 8, pivot // 8]

    def b_piece(col):
        return bg.at[:, col // 2, me.r, pl.ds(pl.multiple_of(col % 2 * 8, 8), 8), :]

    def b_gather(index):
        return lambda source: remote(
            bpc, b_piece(source), bc_s.at[index], bc_r.at[index], (me.r, me.col(*COLUMN[index]))
        )

    for index in range(7):
        b_gather(index)(me.c).start()
    own_b = pltpu.make_async_copy(bpc, b_piece(me.c), own.at[4])
    own_b.start()

    for index, (dy, dk) in enumerate(COLUMN):
        col_spread(index)(me.col(-dy, -dk)).wait_recv()
    for j, pivot in enumerate(pivots):
        cpc[j] = cols[pivot % 8, pivot // 8]

    def c_out(index):
        return lambda source: remote(
            cpc, cg.at[source], c_s.at[index], c_r.at[index], (me.r, me.col(STEP[index], 0))
        )

    def c_swap(which):
        source = me.col(-STEP[which - 1] if which else 0, 0)
        src = cg.at[source] if which else cpc
        return lambda landed: remote(
            src, cg.at[landed], cx_s.at[which], cx_r.at[which], (me.r, me.col(0, 1))
        )

    own_b.wait()
    for index, (dy, dk) in enumerate(COLUMN):
        b_gather(index)(me.col(-dy, -dk)).wait_recv()

    def b_at(pivot):
        return lambda source: bg.at[:, pivot, source]

    b1 = PlaneGather(me, b_at(me.k), b_at(me.k)(me.r), True, True, ba)
    b2 = PlaneGather(me, b_at(2 + me.k), b_at(2 + me.k)(me.r), False, True, bb)
    b1.start()
    b2.start()

    def b_swap(half, slot, source, back):
        pivot = 2 * half + (1 - me.k if back else me.k)
        block = bg.at[:, pivot, source]
        return remote(block, block, bx_s.at[half, slot], bx_r.at[half, slot], (me.r, me.col(0, 1)))

    for gather in (b1, b2):
        gather.forward(0)
    for index in range(3):
        c_out(index)(me.c).start()
    c_swap(0)(me.c).start()
    own_c = pltpu.make_async_copy(cpc, cg.at[me.c], own.at[5])
    own_c.start()

    for gather in (b1, b2):
        gather.relay()
    for which in range(1, 4):
        for half, gather in enumerate((b1, b2)):
            source = gather.forward(which)
            b_swap(half, which - 1, source, False).start()
    for gather in (u1, u2):
        gather.relay()
    for which in range(4):
        for half, gather in enumerate((b1, b2)):
            for index, source in enumerate(gather.relay_second(which)):
                b_swap(half, 3 + which * 3 + index, source, False).start()
    for which in range(4):
        for gather in (u1, u2):
            gather.forward(which)
    for which in range(1, 4):
        source = me.col(-STEP[which - 1], 0)
        c_out(which - 1)(source).wait_recv()
        c_swap(which)(source).start()
    for half, gather in enumerate((b1, b2)):
        for which in range(4):
            source = gather.finish(which)
            b_swap(half, 5 + which * 3, source, False).start()

    def b_arrived(half, gather):
        for which in range(4):
            if which:
                source = gather.number(SHIFT[which], 0)
                b_swap(half, which - 1, source, True).wait_recv()
            for index, shift in enumerate((-1, 1, 2)):
                source = gather.number(SHIFT[which], shift)
                b_swap(half, 3 + which * 3 + index, source, True).wait_recv()

    def u_relay(which):
        for gather in (u1, u2):
            gather.relay_second(which)

    row_tile = (lax.broadcasted_iota(jnp.int32, (512, 1), 0) // 256) * 16 + me.r
    in1 = (row_tile == pivots[0]) | (row_tile == pivots[1])
    in2 = (row_tile == pivots[2]) | (row_tile == pivots[3])

    def b_part(rows, cols):
        return jnp.concatenate(
            [bg[2 * cols + j, pl.ds(2 * rows, 2)].reshape(512, 256) for j in range(2)], axis=1
        )

    def c_part(cols):
        return jnp.concatenate([cg[:, 2 * cols + j].reshape(512, 256) for j in range(2)], axis=1)

    b_arrived(0, b1)
    block[...] = b_part(0, 0)
    invert(block, block_high, block_low, x1)
    b_arrived(1, b2)
    u_relay(0)
    x1_halves = split(x1[...])
    b12 = split(b_part(0, 1))
    t_halves = split(dot3(split(b_part(1, 0)), x1_halves))
    block[...] = b_part(1, 1) - dot3(t_halves, b12)
    u_relay(1)
    own_c.wait()
    for which in range(4):
        c_swap(which)(me.col(-STEP[which - 1] if which else 0, 1)).wait_recv()
    lower = dot3(split(c_part(0)), x1_halves)
    l1[...] = lower
    lower = jnp.where(in1, 0.0, lower)
    c2[...] = c_part(1) - dot3(split(lower), b12)
    u_relay(2)
    u_relay(3)
    invert(block, block_high, block_low, x2)
    lower2 = dot3(split(c2[...]), split(x2[...]))
    l2[...] = lower2
    lower2 = jnp.where(in1 | in2, 0.0, lower2)
    halves = split(lower2)
    lt_high[:, 512:], lt_low[:, 512:] = halves
    lt_high[:, :512], lt_low[:, :512] = split(lower - dot3(halves, t_halves))

    own_u.wait()
    for which in range(4):
        for gather in (u1, u2):
            gather.finish(which)
    for b in range(4):
        update = dot3((lt_high[...], lt_low[...]), split(ug[b].reshape(1024, 256)))
        col_tile = b * 8 + me.c
        new = m[:, b].reshape(512, 256) - update
        for j in range(4):
            window = slice(j % 2 * 256, j % 2 * 256 + 256)
            if j < 2:
                column = jnp.where(in1, cg[:, j].reshape(512, 256), l1[:, window])
            else:
                column = jnp.where(in1 | in2, c2[:, window], l2[:, window])
            new = jnp.where(col_tile == pivots[j], column, new)
        for half in range(2):
            result[pl.ds(2 * b + half, 512, stride=8), :] = new[:, half * 128 : half * 128 + 128]

    written = [
        pltpu.make_async_copy(result.at[pl.ds(512 * i, 512)], out.at[pl.ds(512 * i, 512)], out_sem.at[i])
        for i in range(8)
    ]
    for copy in written:
        copy.start()
    children.drain()
    for index in range(15):
        row_spread(index)(me.r).wait_send()
    for index in range(7):
        col_spread(index)(me.c).wait_send()
        b_scatter(index)(me.c).wait_send()
        b_gather(index)(me.c).wait_send()
    for index in range(3):
        c_out(index)(me.c).wait_send()
    for which in range(4):
        c_swap(which)(me.c).wait_send()
    for gather in (u1, u2, b1, b2):
        gather.drain()
    for half in range(2):
        for slot in range(15):
            b_swap(half, slot, me.r, False).wait_send()
    for copy in written:
        copy.wait()


def eliminate(panel, targets, front, tiles):
    plane = [DMA((4,)), DMA((4,)), DMA((16,)), DMA((16,))]
    square = pltpu.VMEM((512, 512), F32)
    narrow = pltpu.VMEM((512, 512), BF16)
    return pl.pallas_call(
        pivot_kernel,
        name="pivots",
        out_shape=[
            jax.ShapeDtypeStruct((4096, 128), F32),
            jax.ShapeDtypeStruct((16, 8, 128), jnp.int32),
        ],
        in_specs=[SMEM, VMEM, ANY, ANY],
        out_specs=[ANY] * 2,
        scratch_shapes=[
            pltpu.VMEM((16, 256, 256), F32),
            pltpu.VMEM((8, 128), jnp.int32),
            pltpu.VMEM((16, 256, 256), F32),
            pltpu.VMEM((16, 8, 128), jnp.int32),
            pltpu.VMEM((2, 4, 256, 256), F32),
            pltpu.VMEM((4096, 128), F32),
            pltpu.VMEM((4096, 128), F32),
            pltpu.VMEM((16, 2, 4, 16, 256), F32),
            pltpu.VMEM((8, 4, 64, 256), F32),
            pltpu.VMEM((4, 4, 16, 16, 256), F32),
            pltpu.VMEM((4, 4, 16, 16, 256), F32),
            pltpu.VMEM((8, 4, 64, 256), F32),
            pltpu.VMEM((4, 4, 16, 256), F32),
            pltpu.VMEM((4, 64, 256), F32),
            pltpu.VMEM((8, 4, 8, 256), F32),
            pltpu.VMEM((4, 8, 256), F32),
            square, narrow, narrow, square, square, square, square, square,
            pltpu.VMEM((512, 1024), BF16), pltpu.VMEM((512, 1024), BF16),
            DMA((7,)),
            DMA((15,)), DMA((15,)), DMA((7,)), DMA((7,)),
            DMA((7,)), DMA((7,)), DMA((7,)), DMA((7,)),
            DMA((3,)), DMA((3,)), DMA((4,)), DMA((4,)),
            plane, plane, plane, plane,
            DMA((2, 15)), DMA((2, 15)),
            DMA((8,)), [DMA((2,)), DMA((2,))] + [DMA((16,))] * 8,
        ],
        compiler_params=pltpu.CompilerParams(
            collective_id=0, has_side_effects=True, vmem_limit_bytes=56 * 2**20
        ),
    )(panel, targets, front, tiles)[0]


def hand_over_kernel(source, out, held, sems):
    def copies(step):
        refs = ((source, held), (held, out))[step]
        for i in range(8):
            part = pl.ds(4096 // 8 * i, 4096 // 8)
            yield pltpu.make_async_copy(refs[0].at[part], refs[1].at[part], sems.at[step, i])

    for copy in copies(0):
        copy.start()
    for brought, written in zip(copies(0), copies(1)):
        brought.wait()
        written.start()
    for copy in copies(1):
        copy.wait()


def hand_over(result):
    return pl.pallas_call(
        hand_over_kernel,
        name="hand_over",
        out_shape=jax.ShapeDtypeStruct(result.shape, result.dtype),
        in_specs=[ANY],
        out_specs=ANY,
        scratch_shapes=[pltpu.VMEM(result.shape, result.dtype), DMA((2, 8))],
        compiler_params=pltpu.CompilerParams(vmem_limit_bytes=60 * 2**20),
    )(result)


def shards(front_tiles, child_tiles, child_target, panel_tiles):
    result = eliminate(
        panel_tiles,
        child_target.reshape(16, 2).T,
        front_tiles.reshape(4096, 128),
        child_tiles.reshape(16, 256, 256),
    )
    return hand_over(result).reshape(front_tiles.shape)


def solution(mesh):
    in_specs = (
        P(None, "row", None, None, "col", None),
        P("row", "col", None, None, None),
        P("row", "col", None, None),
        P(),
    )
    out_specs = P(None, "row", None, None, "col", None)
    return jax.shard_map(shards, mesh=mesh, in_specs=in_specs, out_specs=out_specs, check_vma=False)
```
